128 devices in a mesh: view: 8 (over y, x_hi), tile: 16 (over z, x_lo, core).
Axes of the slice: x: 4 (x_hi: 2, x_lo: 2; x = x_hi * 2 + x_lo), y: 4, z: 4, core: 2. Of those that a mesh axis runs over, the one named last changes fastest.
Arguments:
- object_band: float32 [16, 2, 1024, 128], P('view', None, 'tile'), may hold values from -6 to 6
- dual_band: float32 [16, 2, 1024, 128], P('view', None, 'tile'), may hold values from -6 to 6
- probe_field: float32 [2, 128, 128], replicated, may hold values from -6 to 6
- positions: int32 [16, 512], P('view', 'tile'), may hold values from 0 to 63
- live_counts: int32 [16, 16], P('view', 'tile'), may hold values from 1 to 32, 170 in all within a row
- photon_counts: int32 [16, 512, 128, 128], P('view', 'tile'), may hold values from 0 to 1023
- footprints: int32 [16, 16], P('view', 'tile'), may hold values from 0 to 14
- weights: bfloat16 [16, 128, 131072], P('view', None, 'tile'), may hold values from -0.046875 to 0.046875
- volume: float32 [2, 1024, 128, 128], P(None, 'tile'), may hold values from -6 to 6
Outputs:
- object_new: float32 [16, 2, 1024, 128], P('view', None, 'tile')
- dual_new: float32 [16, 2, 1024, 128], P('view', None, 'tile')
- volume_new: float32 [2, 1024, 128, 128], P(None, 'tile')
The draws below stay inside these ranges and needn't reach their ends.
Inputs may be any that keep to these rules, and one draw needn't show every extreme that they name: `positions`: offset of a slot's scan position from the first column of the tile that owns the slot. `live_counts`: the first that many of a tile's 32 slots are live; each view has exactly 170 live slots, and in each view some tile has all 32 live. `footprints`: first of the 2 consecutive detector tiles that a volume tile's shadow covers in a view.
All inputs are finite; a program needn't handle non-finite values. No bound on the sum of `live_counts` on one device may be relied on, other than what follows from the above.
Results may differ from the reference program's by a relative error of at most 0.006.
Values may be sent and summed in bfloat16 or wider, within the bound.
A program may use at most 128 MiB of HBM per device.

```python
import math
import jax
import jax.numpy as jnp
import numpy as np
from jax import lax

PW = 128
PH = 128
CAP = 32
NY = 128
FOOT = 2
WT = 64
W = 1024
VIEWS = 16
PATCHES = 170
VOX = 8192
FOOT_COLS = 128
N_TILE = 16


def plant(drawn, stream_key, least, top_value):
    longest = drawn.shape.index(max(drawn.shape))
    spots = []
    for shift in (0, 1):
        where = [jax.random.randint(jax.random.fold_in(stream_key, axis), (), 0, length) for axis, length in enumerate(drawn.shape)]
        where[longest] = (where[longest] + shift) % drawn.shape[longest]
        spots.append(tuple(where))
    return drawn.at[spots[0]].set(least).at[spots[1]].set(top_value)


def levels(stream_key, dims, pieces, low, largest):
    def one(dim, blocks):
        heights = jax.random.uniform(jax.random.fold_in(jax.random.fold_in(stream_key, 6), dim), (blocks,), jnp.float32, low / len(pieces), largest / len(pieces))
        return jnp.repeat(jnp.exp(heights), dims[dim] // blocks).reshape((-1,) + (1,) * (len(dims) - dim - 1))

    level = one(*pieces[0])
    for cut in pieces[1:]:
        level = level * one(*cut)
    return level


def split_up(number_of, total, most, skew):
    loads = [(1 << 20) // math.isqrt(rank ** skew) + 1 for rank in range(2, number_of + 1)]
    spare, holding = total - most - (number_of - 1), [1] * (number_of - 1)
    while spare > 0:
        movable = [i for i in range(number_of - 1) if holding[i] < most]
        mass, remaining = sum([loads[i] for i in movable]), spare
        for i in movable:
            addition = min(most - holding[i], max(1, remaining * loads[i] // mass), spare)
            holding[i] = holding[i] + addition
            spare = spare - addition
    return np.array([most] + holding)


def uneven(key, number_of, total, bound, slope):
    if number_of == 2:
        one = jax.random.randint(key, (), max(1, total - bound), min(bound, total - 1) + 1)
        return jnp.stack([one, total - one])
    lengths = jnp.asarray(split_up(number_of, total, bound, slope), jnp.int32)
    twos = (number_of - 1) // 2
    donor, receiver = lengths[1:1 + 2 * twos:2], lengths[2:2 + 2 * twos:2]
    slack = jnp.minimum(donor - 1, bound - receiver)
    shifted = jax.random.randint(jax.random.fold_in(key, 1), (twos,), 0, 1 << 20) % (slack + 1)
    lengths = lengths.at[1:1 + 2 * twos:2].set(donor - shifted).at[2:2 + 2 * twos:2].set(receiver + shifted)
    return lengths[jax.random.permutation(jax.random.fold_in(key, 2), number_of)]


def bell_draw(key, dims, width, most, pieces=(), kind=jnp.bfloat16):
    values = width * jax.random.normal(key, dims, jnp.float32)
    if pieces:
        values = values * levels(key, dims, pieces, -0.22, 0.18)
    return jnp.clip(values, -most, most).astype(kind)


def setup_inputs(seed: int = 0) -> dict:
    seeds = jax.random.split(jax.random.key(seed), 10)
    object_band = bell_draw(seeds[0], (VIEWS, 2, W, PH), 1.0, 6.0, ((0, 8), (2, 16)), jnp.float32)
    dual_band = bell_draw(seeds[1], (VIEWS, 2, W, PH), 1.0, 6.0, ((0, 8), (2, 16)), jnp.float32)
    probe_field = bell_draw(seeds[2], (2, PW, PH), 1.0, 6.0, (), jnp.float32)
    positions = plant(jax.random.randint(seeds[3], (VIEWS, N_TILE * CAP), 0, WT), jax.random.fold_in(seeds[3], 1), 0, WT - 1).astype(jnp.int32)
    live_counts = jax.vmap(lambda own: uneven(own, N_TILE, PATCHES, CAP, 2))(jax.random.split(seeds[4], VIEWS)).reshape((VIEWS, N_TILE)).astype(jnp.int32)
    photon_counts = plant(jax.random.randint(seeds[5], (VIEWS, N_TILE * CAP, PW, PH), 0, 1024), jax.random.fold_in(seeds[5], 1), 0, 1023).astype(jnp.int32)
    footprints = plant(jax.random.randint(seeds[6], (VIEWS, N_TILE), 0, N_TILE - FOOT + 1), jax.random.fold_in(seeds[6], 1), 0, N_TILE - FOOT).astype(jnp.int32)
    weights = bell_draw(seeds[7], (VIEWS, FOOT_COLS, W * NY), (FOOT * VOX) ** -0.5, 0.046875, ((0, 8), (2, 16)))
    volume = bell_draw(seeds[8], (2, W, NY, PH), 1.0, 6.0, ((1, 16),), jnp.float32)
    return dict(object_band=object_band, dual_band=dual_band, probe_field=probe_field, positions=positions, live_counts=live_counts, photon_counts=photon_counts, footprints=footprints, weights=weights, volume=volume)


rho_weight = 0.5
step_size = 0.5
prior_weight = 0.5
floor_term = 0.25

def tables(order_n):
    counter = jnp.arange(order_n, dtype=jnp.int32)
    phase_index = counter[:, None] * counter[None, :] % order_n
    angles = phase_index.astype(jnp.float32) * (2.0 * jnp.pi / order_n)
    scaling = 1.0 / jnp.sqrt(jnp.float32(order_n))
    return (jnp.cos(angles) * scaling, -jnp.sin(angles) * scaling)

def block_minus(parts):
    upper_half = jnp.concatenate([parts[0], -parts[1]], axis=1)
    lower_half = jnp.concatenate([parts[1], parts[0]], axis=1)
    return jnp.concatenate([upper_half, lower_half], axis=0).astype(jnp.bfloat16)

def block_plus(parts):
    upper_half = jnp.concatenate([parts[0], parts[1]], axis=1)
    lower_half = jnp.concatenate([-parts[1], parts[0]], axis=1)
    return jnp.concatenate([upper_half, lower_half], axis=0).astype(jnp.bfloat16)

def markov(padded):
    centre = padded[:, 1:-1, 1:-1, 1:-1]
    summed = jnp.zeros_like(centre)
    neighbours = (padded[:, 2:, 1:-1, 1:-1], padded[:, :-2, 1:-1, 1:-1], padded[:, 1:-1, 2:, 1:-1], padded[:, 1:-1, :-2, 1:-1], padded[:, 1:-1, 1:-1, 2:], padded[:, 1:-1, 1:-1, :-2])
    for neighbour in neighbours:
        difference = centre - neighbour
        summed = summed + difference / jnp.sqrt(1.0 + difference * difference)
    return summed

def patch_update(window, probe_field, counts_grid, dft_blocks):
    left_a, right_b, right_a, left_b = dft_blocks
    probe_re = probe_field[0]
    probe_im = probe_field[1]
    obj_re = window[0]
    obj_im = window[1]
    exit_wave = jnp.stack([probe_re * obj_re - probe_im * obj_im, probe_re * obj_im + probe_im * obj_re]).astype(jnp.bfloat16)
    num_cols = exit_wave.shape[1]
    num_rows = exit_wave.shape[2]
    columns_done = jnp.dot(left_a, exit_wave.reshape(2 * num_cols, num_rows), preferred_element_type=jnp.float32).astype(jnp.bfloat16)
    columns_done = columns_done.reshape(2, num_cols, num_rows).transpose(1, 0, 2).reshape(num_cols, 2 * num_rows)
    spectrum = jnp.dot(columns_done, right_b, preferred_element_type=jnp.float32)
    amplitude = jnp.sqrt(counts_grid.astype(jnp.float32)) / 16.0
    spec_re = spectrum[:, :num_rows]
    spec_im = spectrum[:, num_rows:]
    factor = amplitude / jnp.sqrt(spec_re * spec_re + spec_im * spec_im + floor_term)
    replaced = (spectrum * jnp.concatenate([factor, factor], axis=1)).astype(jnp.bfloat16)
    inverse_rows = jnp.dot(replaced, right_a, preferred_element_type=jnp.float32).astype(jnp.bfloat16)
    inverse_rows = inverse_rows.reshape(num_cols, 2, num_rows).transpose(1, 0, 2).reshape(2 * num_cols, num_rows)
    new_wave = jnp.dot(left_b, inverse_rows, preferred_element_type=jnp.float32).reshape(2, num_cols, num_rows)
    difference = new_wave - exit_wave.astype(jnp.float32)
    diff_re = difference[0]
    diff_im = difference[1]
    return jnp.stack([probe_re * diff_re + probe_im * diff_im, probe_re * diff_im - probe_im * diff_re, probe_re * probe_re + probe_im * probe_im])

def reference(object_band, dual_band, probe_field, positions, live_counts, photon_counts, footprints, weights, volume):
    dft_blocks = (block_minus(tables(PW)), block_plus(tables(PH)), block_minus(tables(PH)), block_plus(tables(PW)))
    volume_low = volume.astype(jnp.bfloat16).reshape(2, N_TILE, VOX, PH).transpose(1, 2, 0, 3).reshape(N_TILE, VOX, 2 * PH)

    def project_view(entries):
        view_weights, view_foot = entries

        def add_tile(summed, tile_index):
            weight_block = lax.dynamic_slice_in_dim(view_weights, tile_index * VOX, VOX, 1)
            window = jnp.dot(weight_block, volume_low[tile_index], preferred_element_type=jnp.float32)
            window = window.reshape(FOOT_COLS, 2, PH).transpose(1, 0, 2)
            first_col = (view_foot[tile_index] * WT).astype(jnp.int32)
            previous = lax.dynamic_slice_in_dim(summed, first_col, FOOT_COLS, 1)
            return (lax.dynamic_update_slice_in_dim(summed, previous + window, first_col, 1), None)
        summed, _ = lax.scan(add_tile, jnp.zeros((2, W, PH), jnp.float32), jnp.arange(N_TILE, dtype=jnp.int32))
        return summed
    projection = lax.map(project_view, (weights, footprints))

    def view_update(entries):
        obj_view, offsets, view_counts, view_photons = entries
        padded = jnp.pad(obj_view, ((0, 0), (0, 2 * WT), (0, 0)))
        accumulated = jnp.zeros((3, W + 2 * WT, PH), jnp.float32)

        def slot_step(carried, slot_entries):
            slot_index, offset_col, counts_grid = slot_entries
            tile_index = slot_index // CAP
            first_col = (tile_index * WT + offset_col).astype(jnp.int32)
            is_live = slot_index % CAP < view_counts[tile_index]

            def apply_patch(current):
                window = lax.dynamic_slice_in_dim(padded, first_col, PW, 1)
                contrib = patch_update(window, probe_field, counts_grid, dft_blocks)
                previous = lax.dynamic_slice_in_dim(current, first_col, PW, 1)
                return lax.dynamic_update_slice_in_dim(current, previous + contrib, first_col, 1)
            return (lax.cond(is_live, apply_patch, lambda current: current, carried), None)
        slot_indices = jnp.arange(N_TILE * CAP, dtype=jnp.int32)
        accumulated, _ = lax.scan(slot_step, accumulated, (slot_indices, offsets, view_photons))
        return accumulated[:, :W]
    update = lax.map(view_update, (object_band, positions, live_counts, photon_counts))
    object_new = object_band + update[:, 0:2] / (1.0 + update[:, 2:3]) - rho_weight * (object_band - projection - dual_band)
    dual_new = dual_band + projection - object_new
    residual = (projection - object_new + dual_band).astype(jnp.bfloat16)

    def back_tile(tile_index):
        weight_block = lax.dynamic_slice_in_dim(weights, tile_index * VOX, VOX, 2).astype(jnp.float32)
        starts = (footprints[:, tile_index] * WT).astype(jnp.int32)
        windows = jax.vmap(lambda resid_view, first_col: lax.dynamic_slice_in_dim(resid_view, first_col, FOOT_COLS, 1))(residual, starts)
        return jnp.einsum('acx,akch->kxh', weight_block, windows.astype(jnp.float32))
    gradient = lax.map(back_tile, jnp.arange(N_TILE, dtype=jnp.int32))
    gradient = gradient.transpose(1, 0, 2, 3).reshape(2, W, NY, PH)
    half_step = volume - step_size * gradient
    padded_volume = jnp.pad(half_step, ((0, 0), (1, 1), (1, 1), (1, 1)))
    volume_new = half_step - step_size * prior_weight * markov(padded_volume)
    return (object_new, dual_new, volume_new)
```

```python
import functools

import jax
import jax.numpy as jnp
import numpy as np
from jax import lax
from jax.experimental import pallas as pl
from jax.experimental.pallas import tpu as pltpu
from jax.sharding import PartitionSpec as P

rho_weight = 0.5
step_size = 0.5
prior_weight = 0.5
MESH = pl.DeviceIdType.MESH
BATCH = 4
MIB = 2**20


def dft_tables(order):
    counter = np.arange(order)
    angles = ((counter[:, None] * counter[None, :]) % order).astype(np.float32)
    angles = angles * np.float32(2.0 * np.pi / order)
    scaling = np.float32(1.0 / np.sqrt(np.float32(order)))
    re, im = np.cos(angles) * scaling, -np.sin(angles) * scaling
    minus = np.block([[re, -im], [im, re]])
    plus = np.block([[re, im], [-im, re]])
    return jnp.asarray(minus, jnp.bfloat16), jnp.asarray(plus, jnp.bfloat16)


def phi(d):
    return d * lax.rsqrt(1.0 + d * d)


def flag(condition):
    return jnp.where(condition, jnp.float32(1.0), jnp.float32(0.0))


def dot(a, b):
    return jnp.dot(a, b, preferred_element_type=jnp.float32)


def front_kernel(
    nv,
    nt,
    positions,
    live_counts,
    footprints,
    object_hbm,
    dual_hbm,
    probe,
    minus,
    plus,
    counts_hbm,
    weights_hbm,
    volume_hbm,
    object_out,
    dual_out,
    gathered,
    dual_v,
    reach,
    counts_v,
    weights_v,
    volume_v,
    weights_in,
    shadow,
    shadow_out,
    shadow_in,
    patch_tmp,
    power_tmp,
    acc,
    upd_out,
    upd_in,
    resid_full,
    rt,
    grad,
    half,
    halo_out,
    halo_in,
    share,
    local_sem,
    chunk_sem,
    w_send,
    w_recv,
    obj_send,
    obj_recv,
    sh_send,
    sh_recv,
    upd_send,
    upd_recv,
    res_send,
    res_recv,
    rel_send,
    rel_recv,
    rt_send,
    rt_recv,
    halo_send,
    halo_recv,
    ag_send,
    ag_recv,
    ag_local,
):
    v = lax.axis_index("view")
    t = lax.axis_index("tile")
    views, slots = positions.shape
    cols = reach.shape[2] // 3
    depth = volume_hbm.shape[2]
    share_cols = cols // nv
    span = share_cols * depth
    rows = probe.shape[2]
    pw = probe.shape[1]

    def remote(src, dst, send, recv, view, tile):
        return pltpu.make_async_remote_copy(
            src_ref=src,
            dst_ref=dst,
            send_sem=send,
            recv_sem=recv,
            device_id={"view": view, "tile": tile},
            device_id_type=MESH,
        )

    def view_at(k):
        return lax.rem(v + k + nv, nv)

    def tile_at(k):
        return lax.rem(t + k + nt, nt)

    back_v, back_t = view_at(-1), jnp.where(v == 0, tile_at(-1), t)
    fore_v, fore_t = view_at(1), jnp.where(v == nv - 1, tile_at(1), t)

    loads = [
        pltpu.make_async_copy(object_hbm, reach.at[:, :, pl.ds(0, cols), :], local_sem.at[0]),
        pltpu.make_async_copy(dual_hbm, dual_v, local_sem.at[1]),
    ]
    for a in range(views):
        loads.append(
            pltpu.make_async_copy(counts_hbm.at[a], counts_v.at[a], local_sem.at[2 + a])
        )

    def chunk_copies(c):
        first = pl.multiple_of(c * span, span)
        return (
            pltpu.make_async_copy(
                weights_hbm.at[:, :, pl.ds(first, span)],
                weights_v.at[:, :, pl.ds(first, span)],
                chunk_sem.at[0, c],
            ),
            pltpu.make_async_copy(
                volume_hbm.at[:, pl.ds(c * share_cols, share_cols)],
                volume_v.at[:, pl.ds(c * share_cols, share_cols)],
                chunk_sem.at[1, c],
            ),
        )

    loads[0].start()
    for c in range(nv):
        for copy in chunk_copies(c):
            copy.start()
    for copy in loads[1:]:
        copy.start()

    barrier = pltpu.get_barrier_semaphore()

    def greet(view, tile):
        pl.semaphore_signal(
            barrier, inc=1, device_id={"view": view, "tile": tile}, device_id_type=MESH
        )

    for k in range(1, nv):
        greet(view_at(k), t)
    for k in range(1, nt):
        greet(v, tile_at(k))
    greet(back_v, back_t)
    greet(fore_v, fore_t)
    pl.semaphore_wait(barrier, nv + nt)

    object_copies = [
        remote(
            object_hbm,
            reach.at[:, :, pl.ds(k * cols, cols), :],
            obj_send.at[k - 1],
            obj_recv.at[k - 1],
            v,
            tile_at(-k),
        )
        for k in (1, 2)
    ]
    for copy in object_copies:
        copy.start()

    weight_copies = []
    for k in range(1, nv):
        to = view_at(k)
        copy = remote(
            weights_hbm.at[:, :, pl.ds(pl.multiple_of(to * span, span), span)],
            weights_in.at[k - 1],
            w_send.at[k - 1],
            w_recv.at[k - 1],
            to,
            t,
        )
        copy.start()
        weight_copies.append(copy)

    shadow[...] = jnp.zeros_like(shadow)

    def project(c, _):
        for copy in chunk_copies(c):
            copy.wait()
        first = pl.multiple_of(c * span, span)
        left = weights_v[:, :, pl.ds(first, span)].reshape(views * 2 * cols, span)
        block = volume_v[:, pl.ds(c * share_cols, share_cols)].astype(jnp.bfloat16)
        right = jnp.concatenate(
            [block[0].reshape(span, rows), block[1].reshape(span, rows)], axis=1
        )
        shadow[...] += dot(left, right)
        return 0

    lax.fori_loop(0, nv, project, 0)

    foot = [footprints[a, 0] for a in range(views)]

    def shadow_part(a, k, part):
        first = a * 2 * cols + part * cols
        return shadow[first : first + cols, k * rows : (k + 1) * rows]

    def placed(to, a, k):
        return shadow_part(a, k, 0) * flag(foot[a] == to) + shadow_part(a, k, 1) * flag(
            foot[a] + 1 == to
        )

    shadow_copies = []
    for step in range(1, nt):
        to = tile_at(step)
        for a in range(views):
            for k in range(2):
                shadow_out[step - 1, a, k] = placed(to, a, k).astype(jnp.bfloat16)
        copy = remote(
            shadow_out.at[step - 1],
            shadow_in.at[step - 1],
            sh_send.at[step - 1],
            sh_recv.at[step - 1],
            v,
            to,
        )
        copy.start()
        shadow_copies.append(copy)

    probe_re, probe_im = probe[0], probe[1]
    acc[...] = jnp.zeros_like(acc)
    patch_tmp[...] = jnp.zeros_like(patch_tmp)
    power_tmp[...] = jnp.zeros_like(power_tmp)
    power_tmp[cols : cols + pw, :] = probe_re * probe_re + probe_im * probe_im
    for copy in loads[:2]:
        copy.wait()
    for copy in object_copies:
        copy.wait()
    for k in (1, 2):
        inside = flag(t + k < nt)
        for a in range(views):
            for plane in range(2):
                reach[a, plane, k * cols : (k + 1) * cols, :] = (
                    reach[a, plane, k * cols : (k + 1) * cols, :] * inside
                )

    def patches(a, b):
        base = b * BATCH
        offsets = [positions[a, base + j] for j in range(BATCH)]
        live_count = live_counts[a, 0]
        lives = [flag(base + j < live_count) for j in range(BATCH)]
        re, im = probe[0], probe[1]
        exits = []
        for j in range(BATCH):
            obj_re = reach[a, 0, pl.ds(offsets[j], pw), :]
            obj_im = reach[a, 1, pl.ds(offsets[j], pw), :]
            exits.append(
                jnp.concatenate(
                    [re * obj_re - im * obj_im, re * obj_im + im * obj_re], axis=0
                ).astype(jnp.bfloat16)
            )
        done = dot(minus[...], jnp.concatenate(exits, axis=1)).astype(jnp.bfloat16)
        done = jnp.concatenate(
            [
                jnp.concatenate(
                    [
                        done[:pw, j * rows : (j + 1) * rows],
                        done[pw:, j * rows : (j + 1) * rows],
                    ],
                    axis=1,
                )
                for j in range(BATCH)
            ],
            axis=0,
        )
        spectrum = dot(done, plus[...])
        s_re, s_im = spectrum[:, :rows], spectrum[:, rows:]
        counts = counts_v[a, pl.ds(base, BATCH)].astype(jnp.float32).reshape(BATCH * pw, rows)
        power = 256.0 * (s_re * s_re + s_im * s_im) + 64.0
        factor = counts * lax.rsqrt(jnp.maximum(counts * power, 1e-20))
        replaced = jnp.concatenate([s_re * factor, s_im * factor], axis=1).astype(jnp.bfloat16)
        inverse = dot(replaced, minus[...]).astype(jnp.bfloat16)
        inverse = jnp.concatenate(
            [
                jnp.concatenate(
                    [
                        inverse[j * pw : (j + 1) * pw, :rows],
                        inverse[j * pw : (j + 1) * pw, rows:],
                    ],
                    axis=0,
                )
                for j in range(BATCH)
            ],
            axis=1,
        )
        wave = dot(plus[...], inverse)
        for j in range(BATCH):
            diff = wave[:, j * rows : (j + 1) * rows] - exits[j].astype(jnp.float32)
            d_re, d_im = diff[:pw] * lives[j], diff[pw:] * lives[j]
            patch_tmp[j, 0, cols : cols + pw, :] = re * d_re + im * d_im
            patch_tmp[j, 1, cols : cols + pw, :] = re * d_im - im * d_re
        for plane in range(2):
            total = acc[a, plane]
            for j in range(BATCH):
                total = total + patch_tmp[j, plane, pl.ds(cols - offsets[j], 3 * cols), :]
            acc[a, plane] = total
        total = acc[a, 2]
        for j in range(BATCH):
            total = total + power_tmp[pl.ds(cols - offsets[j], 3 * cols), :] * lives[j]
        acc[a, 2] = total

    update_copies = []
    for a in range(views):
        loads[2 + a].wait()
        lax.fori_loop(0, slots // BATCH, lambda b, _, a=a: (patches(a, b), 0)[1], 0)
        for k in (1, 2):
            upd_out[a, k - 1] = acc[a, :, k * cols : (k + 1) * cols, :].astype(jnp.bfloat16)
            copy = remote(
                upd_out.at[a, k - 1],
                upd_in.at[a, k - 1],
                upd_send.at[a, k - 1],
                upd_recv.at[a, k - 1],
                v,
                tile_at(k),
            )
            copy.start()
            update_copies.append(copy)

    for copy in shadow_copies:
        copy.wait()
    for copy in update_copies:
        copy.wait()
    from_one, from_two = flag(t >= 1), flag(t >= 2)
    for a in range(views):
        upd = (
            acc[a, :, :cols, :]
            + upd_in[a, 0].astype(jnp.float32) * from_one
            + upd_in[a, 1].astype(jnp.float32) * from_two
        )
        scale = 1.0 / (1.0 + upd[2])
        for k in range(2):
            projection = placed(t, a, k)
            for step in range(1, nt):
                projection = projection + shadow_in[step - 1, a, k].astype(jnp.float32)
            obj = reach[a, k, :cols, :]
            dual = dual_v[a, k]
            new = obj + upd[k] * scale - rho_weight * (obj - projection - dual)
            object_out[a, k] = new
            dual_new = dual + projection - new
            dual_out[a, k] = dual_new
            resid_full[t, a, k] = dual_new.astype(jnp.bfloat16)

    core = lax.rem(t, 2)
    sibling = t + 1 - 2 * core
    chips = nt // 2
    resid_copies = [
        remote(
            resid_full.at[t],
            resid_full.at[t],
            res_send.at[m],
            res_recv.at[m],
            v,
            tile_at(2 * m) if m else sibling,
        )
        for m in range(chips)
    ]
    for copy in resid_copies[1:]:
        copy.start()
    resid_copies[0].start()
    relays = []
    for m in range(1, chips):
        source = tile_at(-2 * m)
        remote(
            resid_full.at[source],
            resid_full.at[source],
            res_send.at[m],
            res_recv.at[m],
            v,
            source,
        ).wait_recv()
        relay = remote(
            resid_full.at[source],
            resid_full.at[source],
            rel_send.at[m - 1],
            rel_recv.at[m - 1],
            v,
            sibling,
        )
        relay.start()
        relays.append(relay)
    remote(
        resid_full.at[sibling], resid_full.at[sibling], res_send.at[0], res_recv.at[0], v, sibling
    ).wait_recv()
    for m in range(1, chips):
        source = lax.rem(sibling - 2 * m + nt, nt)
        remote(
            resid_full.at[source],
            resid_full.at[source],
            rel_send.at[m - 1],
            rel_recv.at[m - 1],
            v,
            sibling,
        ).wait_recv()
    for copy in resid_copies + relays:
        copy.wait_send()

    for a in range(views):
        for k in range(2):
            window = jnp.concatenate([resid_full[foot[a], a, k], resid_full[foot[a] + 1, a, k]], axis=0)
            rt[0, k * rows : (k + 1) * rows, a * 2 * cols : (a + 1) * 2 * cols] = (
                window.astype(jnp.float32).T.astype(jnp.bfloat16)
            )
    rt_copies = []
    for k in range(1, nv):
        copy = remote(rt.at[0], rt.at[k], rt_send.at[k - 1], rt_recv.at[k - 1], view_at(k), t)
        copy.start()
        rt_copies.append(copy)

    own = weights_v[:, :, pl.ds(pl.multiple_of(v * span, span), span)]
    grad[...] = dot(rt[0], own.reshape(views * 2 * cols, span))
    for k in range(1, nv):
        weight_copies[k - 1].wait()
        rt_copies[k - 1].wait()
        grad[...] += dot(rt[k], weights_in[k - 1].reshape(views * 2 * cols, span))

    for c in range(share_cols):
        for k in range(2):
            part = grad[k * rows : (k + 1) * rows, c * depth : (c + 1) * depth].T
            half[k, c] = volume_v[k, v * share_cols + c] - step_size * part

    for k in range(2):
        halo_out[0, k] = half[k, 0].astype(jnp.bfloat16)
        halo_out[1, k] = half[k, share_cols - 1].astype(jnp.bfloat16)
    halo_copies = [
        remote(halo_out.at[0], halo_in.at[1], halo_send.at[0], halo_recv.at[1], back_v, back_t),
        remote(halo_out.at[1], halo_in.at[0], halo_send.at[1], halo_recv.at[0], fore_v, fore_t),
    ]
    for copy in halo_copies:
        copy.start()

    row = lax.broadcasted_iota(jnp.int32, (depth, rows), 0)
    lane = lax.broadcasted_iota(jnp.int32, (depth, rows), 1)

    def inner(x):
        below = jnp.where(row == 0, 0.0, pltpu.roll(x, 1, 0))
        above = jnp.where(row == depth - 1, 0.0, pltpu.roll(x, depth - 1, 0))
        left = jnp.where(lane == 0, 0.0, pltpu.roll(x, 1, 1))
        right = jnp.where(lane == rows - 1, 0.0, pltpu.roll(x, rows - 1, 1))
        return phi(x - below) + phi(x - above) + phi(x - left) + phi(x - right)

    def finish(k, c, before, after):
        x = half[k, c]
        prior = inner(x) + phi(x - before) + phi(x - after)
        share[k, c] = (x - (step_size * prior_weight) * prior).astype(jnp.bfloat16)

    for k in range(2):
        lax.fori_loop(
            1,
            share_cols - 1,
            lambda c, _, k=k: (finish(k, c, half[k, c - 1], half[k, c + 1]), 0)[1],
            0,
        )
    for copy in halo_copies:
        copy.wait()
    has_back = flag((v > 0) | (t > 0))
    has_fore = flag((v < nv - 1) | (t < nt - 1))
    for k in range(2):
        finish(k, 0, halo_in[0, k].astype(jnp.float32) * has_back, half[k, 1])
        finish(
            k,
            share_cols - 1,
            half[k, share_cols - 2],
            halo_in[1, k].astype(jnp.float32) * has_fore,
        )

    ag_copies = []
    for k in range(1, nv):
        copy = remote(
            share, gathered.at[v], ag_send.at[k - 1], ag_recv.at[k - 1], view_at(k), t
        )
        copy.start()
        ag_copies.append(copy)
    own_copy = pltpu.make_async_copy(share, gathered.at[v], ag_local)
    own_copy.start()
    for k in range(1, nv):
        source = view_at(-k)
        remote(
            share, gathered.at[source], ag_send.at[k - 1], ag_recv.at[k - 1], source, t
        ).wait_recv()
    for copy in ag_copies:
        copy.wait_send()
    own_copy.wait()


def widen_kernel(x_ref, o_ref):
    o_ref[...] = x_ref[0].astype(jnp.float32)


def per_device(
    nv,
    nt,
    object_band,
    dual_band,
    probe_field,
    positions,
    live_counts,
    photon_counts,
    footprints,
    weights,
    volume,
):
    views, _, cols, rows = object_band.shape
    pw = probe_field.shape[1]
    slots = positions.shape[1]
    depth = volume.shape[2]
    share_cols = cols // nv
    span = share_cols * depth
    minus, plus = dft_tables(pw)
    any_space = pl.BlockSpec(memory_space=pl.ANY)
    smem = pl.BlockSpec(memory_space=pltpu.SMEM)
    vmem = pl.BlockSpec(memory_space=pltpu.VMEM)
    bf16, f32 = jnp.bfloat16, jnp.float32
    dma = pltpu.SemaphoreType.DMA
    chips = nt // 2
    band = jax.ShapeDtypeStruct(object_band.shape, f32)
    object_new, dual_new, gathered = pl.pallas_call(
        functools.partial(front_kernel, nv, nt),
        out_shape=(
            band,
            band,
            jax.ShapeDtypeStruct((nv, 2, share_cols, depth, rows), bf16),
        ),
        in_specs=[smem] * 3 + [any_space] * 2 + [vmem] * 3 + [any_space] * 3,
        out_specs=(vmem, vmem, any_space),
        scratch_shapes=[
            pltpu.VMEM((views, 2, cols, rows), f32),
            pltpu.VMEM((views, 2, 3 * cols, rows), f32),
            pltpu.VMEM((views, slots, pw, rows), jnp.int32),
            pltpu.VMEM(weights.shape, bf16),
            pltpu.VMEM(volume.shape, f32),
            pltpu.VMEM((nv - 1, views, 2 * cols, span), bf16),
            pltpu.VMEM((views * 2 * cols, 2 * rows), f32),
            pltpu.VMEM((nt - 1, views, 2, cols, rows), bf16),
            pltpu.VMEM((nt - 1, views, 2, cols, rows), bf16),
            pltpu.VMEM((BATCH, 2, 4 * cols, rows), f32),
            pltpu.VMEM((4 * cols, rows), f32),
            pltpu.VMEM((views, 3, 3 * cols, rows), f32),
            pltpu.VMEM((views, 2, 3, cols, rows), bf16),
            pltpu.VMEM((views, 2, 3, cols, rows), bf16),
            pltpu.VMEM((nt, views, 2, cols, rows), bf16),
            pltpu.VMEM((nv, 2 * rows, views * 2 * cols), bf16),
            pltpu.VMEM((2 * rows, span), f32),
            pltpu.VMEM((2, share_cols, depth, rows), f32),
            pltpu.VMEM((2, 2, depth, rows), bf16),
            pltpu.VMEM((2, 2, depth, rows), bf16),
            pltpu.VMEM((2, share_cols, depth, rows), bf16),
            dma((2 + views,)),
            dma((2, nv)),
            dma((nv - 1,)),
            dma((nv - 1,)),
            dma((2,)),
            dma((2,)),
            dma((nt - 1,)),
            dma((nt - 1,)),
            dma((views, 2)),
            dma((views, 2)),
            dma((chips,)),
            dma((chips,)),
            dma((chips - 1,)),
            dma((chips - 1,)),
            dma((nv - 1,)),
            dma((nv - 1,)),
            dma((2,)),
            dma((2,)),
            dma((nv - 1,)),
            dma((nv - 1,)),
            dma(()),
        ],
        compiler_params=pltpu.CompilerParams(
            collective_id=0, has_side_effects=True, vmem_limit_bytes=52 * MIB
        ),
        name="front",
    )(
        positions,
        live_counts,
        footprints,
        object_band,
        dual_band,
        probe_field,
        minus,
        plus,
        photon_counts,
        weights,
        volume,
    )
    volume_new = pl.pallas_call(
        widen_kernel,
        grid=(nv,),
        out_shape=jax.ShapeDtypeStruct(volume.shape, f32),
        in_specs=[pl.BlockSpec((1, 2, share_cols, depth, rows), lambda i: (i, 0, 0, 0, 0))],
        out_specs=pl.BlockSpec((2, share_cols, depth, rows), lambda i: (0, i, 0, 0)),
        compiler_params=pltpu.CompilerParams(vmem_limit_bytes=32 * MIB),
        name="widen",
    )(gathered)
    return object_new, dual_new, volume_new


def solution(mesh):
    return jax.shard_map(
        functools.partial(per_device, mesh.shape["view"], mesh.shape["tile"]),
        mesh=mesh,
        in_specs=(
            P("view", None, "tile", None),
            P("view", None, "tile", None),
            P(),
            P("view", "tile"),
            P("view", "tile"),
            P("view", "tile", None, None),
            P("view", "tile"),
            P("view", None, "tile"),
            P(None, "tile", None, None),
        ),
        out_specs=(
            P("view", None, "tile", None),
            P("view", None, "tile", None),
            P(None, "tile", None, None),
        ),
        check_vma=False,
    )
```

```python
import functools

import jax
import jax.numpy as jnp
import numpy as np
from jax import lax
from jax.experimental import pallas as pl
from jax.experimental.pallas import tpu as pltpu
from jax.sharding import PartitionSpec as P

rho_weight = 0.5
step_size = 0.5
prior_weight = 0.5
MESH = pl.DeviceIdType.MESH
BATCH = 4
FRONT_VMEM = 60
WIDEN_VMEM = 60
PUMP = (11, 4, 2, 4, 4, 4, 4, 4)
MIB = 2**20


def dft_tables(order):
    counter = np.arange(order)
    angles = ((counter[:, None] * counter[None, :]) % order).astype(np.float32)
    angles = angles * np.float32(2.0 * np.pi / order)
    scaling = np.float32(1.0 / np.sqrt(np.float32(order)))
    re, im = np.cos(angles) * scaling, -np.sin(angles) * scaling
    minus = np.block([[re, -im], [im, re]])
    plus = np.block([[re, im], [-im, re]])
    return jnp.asarray(minus, jnp.bfloat16), jnp.asarray(plus, jnp.bfloat16)


def phi(d):
    return d * lax.rsqrt(1.0 + d * d)


def flag(condition):
    return jnp.where(condition, jnp.float32(1.0), jnp.float32(0.0))


def dot(a, b):
    return jnp.dot(a, b, preferred_element_type=jnp.float32)


def front_kernel(
    nv,
    nt,
    positions,
    live_counts,
    footprints,
    object_hbm,
    dual_hbm,
    probe_hbm,
    minus_hbm,
    plus_hbm,
    counts_hbm,
    weights_hbm,
    volume_hbm,
    object_out,
    dual_out,
    gathered,
    probe,
    minus,
    plus,
    dual_v,
    reach,
    counts_v,
    weights_v,
    volume_v,
    weights_in,
    shadow,
    shadow_out,
    shadow_in,
    shared_out,
    shared_in,
    patch_tmp,
    power_tmp,
    acc,
    upd_out,
    upd_in,
    resid_first,
    resid_second,
    rt,
    grad,
    half,
    halo_out,
    halo_in,
    share,
    local_sem,
    chunk_sem,
    w_send,
    w_recv,
    obj_send,
    obj_recv,
    sh_send,
    sh_recv,
    gr_send,
    gr_recv,
    upd_send,
    upd_recv,
    res_send,
    res_recv,
    rel_send,
    rel_recv,
    rt_send,
    rt_recv,
    halo_send,
    halo_recv,
    ag_send,
    ag_recv,
):
    v = lax.axis_index("view")
    t = lax.axis_index("tile")
    views, slots = positions.shape
    resid_full = (resid_first, resid_second)
    cols = reach.shape[2] // 3
    depth = volume_hbm.shape[2]
    share_cols = cols // nv
    span = share_cols * depth
    rows = probe.shape[2]
    pw = probe.shape[1]

    def remote(src, dst, send, recv, view, tile):
        return pltpu.make_async_remote_copy(
            src_ref=src,
            dst_ref=dst,
            send_sem=send,
            recv_sem=recv,
            device_id={"view": view, "tile": tile},
            device_id_type=MESH,
        )

    def view_at(k):
        return lax.rem(v + k + nv, nv)

    def tile_at(k):
        return lax.rem(t + k + nt, nt)

    group = 4
    levels = nt // group
    z, place = t // group, lax.rem(t, group)
    core = lax.rem(t, 2)
    sibling = t + 1 - 2 * core
    beside = t + 2 - 4 * (place // 2)
    view_x = lax.rem(v, 2)
    over = v + 1 - 2 * view_x

    def level_at(k):
        return lax.rem(z + k + levels, levels)

    back_v, back_t = view_at(-1), jnp.where(v == 0, tile_at(-1), t)
    fore_v, fore_t = view_at(1), jnp.where(v == nv - 1, tile_at(1), t)

    loads = [
        pltpu.make_async_copy(object_hbm, reach.at[:, :, pl.ds(0, cols), :], local_sem.at[0]),
        pltpu.make_async_copy(dual_hbm, dual_v, local_sem.at[1]),
    ]
    for a in range(views):
        loads.append(
            pltpu.make_async_copy(counts_hbm.at[a], counts_v.at[a], local_sem.at[2 + a])
        )
    for i, (source, target) in enumerate(
        ((probe_hbm, probe), (minus_hbm, minus), (plus_hbm, plus))
    ):
        loads.append(pltpu.make_async_copy(source, target, local_sem.at[2 + views + i]))

    def chunk_copies(c):
        first = pl.multiple_of(c * span, span)
        return (
            pltpu.make_async_copy(
                weights_hbm.at[:, :, pl.ds(first, span)],
                weights_v.at[:, :, pl.ds(first, span)],
                chunk_sem.at[0, c],
            ),
            pltpu.make_async_copy(
                volume_hbm.at[:, pl.ds(c * share_cols, share_cols)],
                volume_v.at[:, pl.ds(c * share_cols, share_cols)],
                chunk_sem.at[1, c],
            ),
        )

    loads[0].start()
    for c in range(nv):
        for copy in chunk_copies(c):
            copy.start()
    for copy in loads[1:]:
        copy.start()

    barrier = pltpu.get_barrier_semaphore()

    def greet(view, tile):
        pl.semaphore_signal(
            barrier, inc=1, device_id={"view": view, "tile": tile}, device_id_type=MESH
        )

    for k in range(1, nv):
        greet(view_at(k), t)
    for k in range(1, nt):
        greet(v, tile_at(k))
    greet(back_v, back_t)
    greet(fore_v, fore_t)
    pl.semaphore_wait(barrier, nv + nt)

    object_copies = [
        remote(
            object_hbm,
            reach.at[:, :, pl.ds(k * cols, cols), :],
            obj_send.at[k - 1],
            obj_recv.at[k - 1],
            v,
            tile_at(-k),
        )
        for k in (1, 2)
    ]
    for copy in object_copies:
        copy.start()

    peers = nv - 1
    piece_rows = 32
    per_view = 2 * cols // piece_rows
    pieces = peers * views * per_view

    def pump(first, count):
        for extra in range(count):
            index = first + extra
            k = index % peers
            row_block = index // peers
            a = row_block // per_view
            rows_at = pl.multiple_of((row_block % per_view) * piece_rows, piece_rows)
            lane = k + 1
            to = lax.rem(v - view_x + 2 * (lane // 2), nv) + lax.rem(view_x + lane, 2)
            remote(
                weights_hbm.at[a, pl.ds(rows_at, piece_rows), pl.ds(pl.multiple_of(to * span, span), span)],
                weights_in.at[k, a, pl.ds(rows_at, piece_rows), :],
                w_send.at[k],
                w_recv.at[k],
                to,
                t,
            ).start()

    pumped = 0

    def pump_some(count):
        nonlocal pumped
        count = min(count, pieces - pumped)
        pump(pumped, count)
        pumped += count

    pump_some(PUMP[0])

    shadow[...] = jnp.zeros_like(shadow)

    def project(c, _):
        for copy in chunk_copies(c):
            copy.wait()
        first = pl.multiple_of(c * span, span)
        left = weights_v[:, :, pl.ds(first, span)].reshape(views * 2 * cols, span)
        block = volume_v[:, pl.ds(c * share_cols, share_cols)].astype(jnp.bfloat16)
        right = jnp.concatenate(
            [block[0].reshape(span, rows), block[1].reshape(span, rows)], axis=1
        )
        shadow[...] += dot(left, right)
        return 0

    lax.fori_loop(0, nv, project, 0)

    foot = [footprints[a] for a in range(views)]

    def shadow_part(a, k, part):
        first = a * 2 * cols + part * cols
        return shadow[first : first + cols, k * rows : (k + 1) * rows]

    def placed(to, a, k):
        return shadow_part(a, k, 0) * flag(foot[a] == to) + shadow_part(a, k, 1) * flag(
            foot[a] + 1 == to
        )

    def level_copy(k):
        return remote(
            shadow_out.at[k - 1],
            shadow_in.at[k - 1],
            sh_send.at[k - 1],
            sh_recv.at[k - 1],
            v,
            level_at(k) * group + place,
        )

    def group_copy(k):
        return remote(
            shared_out.at[k - 1],
            shared_in.at[k - 1],
            gr_send.at[k - 1],
            gr_recv.at[k - 1],
            v,
            z * group + lax.rem(place + k, group),
        )

    for step in range(1, levels):
        for k in range(group):
            to = level_at(step) * group + k
            for a in range(views):
                for plane in range(2):
                    shadow_out[step - 1, k, a, plane] = placed(to, a, plane).astype(jnp.bfloat16)
        level_copy(step).start()

    def level_sum(to, k, a, plane):
        total = placed(to, a, plane)
        for step in range(1, levels):
            total = total + shadow_in[step - 1, k, a, plane].astype(jnp.float32)
        return total

    def share_sums():
        for step in range(1, levels):
            level_copy(step).wait()
        for step in range(1, group):
            k = lax.rem(place + step, group)
            for a in range(views):
                for plane in range(2):
                    shared_out[step - 1, a, plane] = level_sum(
                        z * group + k, k, a, plane
                    ).astype(jnp.bfloat16)
            group_copy(step).start()

    pump_some(PUMP[1])

    for copy in loads[2 + views :]:
        copy.wait()
    probe_re, probe_im = probe[0], probe[1]
    acc[...] = jnp.zeros_like(acc)
    patch_tmp[...] = jnp.zeros_like(patch_tmp)
    power_tmp[...] = jnp.zeros_like(power_tmp)
    power_tmp[cols : cols + pw, :] = probe_re * probe_re + probe_im * probe_im
    for copy in loads[:2]:
        copy.wait()
    for copy in object_copies:
        copy.wait()
    for k in (1, 2):
        inside = flag(t + k < nt)
        for a in range(views):
            for plane in range(2):
                reach[a, plane, k * cols : (k + 1) * cols, :] = (
                    reach[a, plane, k * cols : (k + 1) * cols, :] * inside
                )

    def patches(a, b):
        base = b * BATCH
        offsets = [positions[a, base + j] for j in range(BATCH)]
        live_count = live_counts[a]
        lives = [flag(base + j < live_count) for j in range(BATCH)]
        re, im = probe[0], probe[1]
        exits = []
        for j in range(BATCH):
            obj_re = reach[a, 0, pl.ds(offsets[j], pw), :]
            obj_im = reach[a, 1, pl.ds(offsets[j], pw), :]
            exits.append(
                jnp.concatenate(
                    [re * obj_re - im * obj_im, re * obj_im + im * obj_re], axis=0
                ).astype(jnp.bfloat16)
            )
        done = dot(minus[...], jnp.concatenate(exits, axis=1)).astype(jnp.bfloat16)
        done = jnp.concatenate(
            [
                jnp.concatenate(
                    [
                        done[:pw, j * rows : (j + 1) * rows],
                        done[pw:, j * rows : (j + 1) * rows],
                    ],
                    axis=1,
                )
                for j in range(BATCH)
            ],
            axis=0,
        )
        spectrum = dot(done, plus[...])
        s_re, s_im = spectrum[:, :rows], spectrum[:, rows:]
        counts = counts_v[a, pl.ds(base, BATCH)].astype(jnp.float32).reshape(BATCH * pw, rows)
        power = 256.0 * (s_re * s_re + s_im * s_im) + 64.0
        factor = counts * lax.rsqrt(jnp.maximum(counts * power, 1e-20))
        replaced = jnp.concatenate([s_re * factor, s_im * factor], axis=1).astype(jnp.bfloat16)
        inverse = dot(replaced, minus[...]).astype(jnp.bfloat16)
        inverse = jnp.concatenate(
            [
                jnp.concatenate(
                    [
                        inverse[j * pw : (j + 1) * pw, :rows],
                        inverse[j * pw : (j + 1) * pw, rows:],
                    ],
                    axis=0,
                )
                for j in range(BATCH)
            ],
            axis=1,
        )
        wave = dot(plus[...], inverse)
        for j in range(BATCH):
            diff = wave[:, j * rows : (j + 1) * rows] - exits[j].astype(jnp.float32)
            d_re, d_im = diff[:pw] * lives[j], diff[pw:] * lives[j]
            patch_tmp[j, 0, cols : cols + pw, :] = re * d_re + im * d_im
            patch_tmp[j, 1, cols : cols + pw, :] = re * d_im - im * d_re
        for plane in range(2):
            total = acc[a, plane]
            for j in range(BATCH):
                total = total + patch_tmp[j, plane, pl.ds(cols - offsets[j], 3 * cols), :]
            acc[a, plane] = total
        total = acc[a, 2]
        for j in range(BATCH):
            total = total + power_tmp[pl.ds(cols - offsets[j], 3 * cols), :] * lives[j]
        acc[a, 2] = total

    def update_copy(a, k):
        return remote(
            upd_out.at[a, k - 1],
            upd_in.at[a, k - 1],
            upd_send.at[a, k - 1],
            upd_recv.at[a, k - 1],
            v,
            tile_at(k),
        )

    def run_patches(a, first, last):
        nonlocal pumped
        each = min(PUMP[2], (pieces - pumped) // (last - first))
        base = pumped

        def body(b, _):
            pump(base + (b - first) * each, each)
            patches(a, b)
            return 0

        lax.fori_loop(first, last, body, 0)
        pumped += each * (last - first)

    def send_update(a):
        for k in (1, 2):
            upd_out[a, k - 1] = acc[a, :, k * cols : (k + 1) * cols, :].astype(jnp.bfloat16)
            update_copy(a, k).start()

    from_one, from_two = flag(t >= 1), flag(t >= 2)

    def finish_object(a):
        for k in (1, 2):
            update_copy(a, k).wait()
        upd = (
            acc[a, :, :cols, :]
            + upd_in[a, 0].astype(jnp.float32) * from_one
            + upd_in[a, 1].astype(jnp.float32) * from_two
        )
        scale = 1.0 / (1.0 + upd[2])
        for k in range(2):
            projection = level_sum(t, place, a, k)
            for step in range(1, group):
                projection = projection + shared_in[step - 1, a, k].astype(jnp.float32)
            obj = reach[a, k, :cols, :]
            dual = dual_v[a, k]
            new = obj + upd[k] * scale - rho_weight * (obj - projection - dual)
            object_out[a, k] = new
            dual_new = dual + projection - new
            dual_out[a, k] = dual_new
            resid_full[a][t, k] = dual_new.astype(jnp.bfloat16)

    def source_at(lane, tile):
        k, j = lane // 2, lane % 2
        base = lax.rem(tile // group - k + levels, levels) * group
        spot = lax.rem(tile, group)
        return base + (lax.rem(spot + 2, group) if j else spot)

    lanes = 2 * levels

    def resid_copy(a, lane, source, to):
        return remote(
            resid_full[a].at[source],
            resid_full[a].at[source],
            res_send.at[a, lane],
            res_recv.at[a, lane],
            v,
            to,
        )

    def relay_copy(a, lane, source):
        return remote(
            resid_full[a].at[source],
            resid_full[a].at[source],
            rel_send.at[a, lane],
            rel_recv.at[a, lane],
            v,
            sibling,
        )

    def send_resid(a):
        resid_copy(a, 1, t, beside).start()
        for k in range(1, levels):
            resid_copy(a, 2 * k, t, level_at(k) * group + place).start()
        relay_copy(a, 0, t).start()

    def relay_resid(a):
        resid_copy(a, 1, beside, beside).wait_recv()
        for k in range(1, levels):
            resid_copy(a, 2 * k + 1, beside, level_at(k) * group + place).start()
        relay_copy(a, 1, beside).start()
        for lane in range(2, lanes):
            source = source_at(lane, t)
            resid_copy(a, lane, source, t).wait_recv()
            relay_copy(a, lane, source).start()

    def rt_part(k, a):
        return rt.at[k, :, pl.ds(a * 2 * cols, 2 * cols)]

    def rt_copy(a, lane, k, to):
        return remote(
            rt_part(k, a),
            rt_part(lane, a),
            rt_send.at[a, lane - 1],
            rt_recv.at[a, lane - 1],
            to,
            t,
        )

    def spread_windows(a):
        rt_copy(a, 1, 1, over).wait_recv()
        for k in range(1, nv // 2):
            rt_copy(a, 2 * k + 1, 1, view_at(2 * k)).start()

    def send_windows(a):
        for lane in range(lanes):
            relay_copy(a, lane, source_at(lane, sibling)).wait_recv()
            relay_copy(a, lane, source_at(lane, t)).wait_send()
        for lane in range(1, lanes):
            resid_copy(a, lane, t, t).wait_send()
        for k in range(2):
            window = jnp.concatenate(
                [resid_full[a][foot[a], k], resid_full[a][foot[a] + 1, k]], axis=0
            )
            rt[0, k * rows : (k + 1) * rows, a * 2 * cols : (a + 1) * 2 * cols] = (
                window.astype(jnp.float32).T.astype(jnp.bfloat16)
            )
        rt_copy(a, 1, 0, over).start()
        for k in range(1, nv // 2):
            rt_copy(a, 2 * k, 0, view_at(2 * k)).start()

    batches = slots // BATCH
    loads[2].wait()
    run_patches(0, 0, batches)
    send_update(0)
    pump_some(PUMP[3])
    share_sums()
    loads[3].wait()
    run_patches(1, 0, batches // 2)
    for step in range(1, group):
        group_copy(step).wait()
    finish_object(0)
    send_resid(0)
    pump_some(PUMP[4])
    run_patches(1, batches // 2, batches)
    send_update(1)
    pump_some(PUMP[5])
    relay_resid(0)
    send_windows(0)
    pump_some(PUMP[6])
    spread_windows(0)
    finish_object(1)
    send_resid(1)
    pump_some(PUMP[7])
    relay_resid(1)
    send_windows(1)
    pump_some(pieces)
    spread_windows(1)

    own = weights_v[:, :, pl.ds(pl.multiple_of(v * span, span), span)]
    grad[...] = dot(rt[0], own.reshape(views * 2 * cols, span))
    for lane in range(1, nv):
        for a in range(views):
            if lane > 1:
                rt_copy(a, lane, 0, v).wait_recv()
            rt_copy(a, lane, 0, v).wait_send()
        k = lane
        remote(
            weights_hbm.at[:, :, pl.ds(0, span)],
            weights_in.at[k - 1],
            w_send.at[k - 1],
            w_recv.at[k - 1],
            view_at(k),
            t,
        ).wait()
        grad[...] += dot(rt[lane], weights_in[k - 1].reshape(views * 2 * cols, span))

    for c in range(share_cols):
        for k in range(2):
            part = grad[k * rows : (k + 1) * rows, c * depth : (c + 1) * depth].T
            half[k, c] = volume_v[k, v * share_cols + c] - step_size * part

    for k in range(2):
        halo_out[0, k] = half[k, 0].astype(jnp.bfloat16)
        halo_out[1, k] = half[k, share_cols - 1].astype(jnp.bfloat16)
    halo_copies = [
        remote(halo_out.at[0], halo_in.at[1], halo_send.at[0], halo_recv.at[1], back_v, back_t),
        remote(halo_out.at[1], halo_in.at[0], halo_send.at[1], halo_recv.at[0], fore_v, fore_t),
    ]
    for copy in halo_copies:
        copy.start()

    row = lax.broadcasted_iota(jnp.int32, (depth, rows), 0)
    lane = lax.broadcasted_iota(jnp.int32, (depth, rows), 1)

    def inner(x):
        below = jnp.where(row == 0, 0.0, pltpu.roll(x, 1, 0))
        above = jnp.where(row == depth - 1, 0.0, pltpu.roll(x, depth - 1, 0))
        left = jnp.where(lane == 0, 0.0, pltpu.roll(x, 1, 1))
        right = jnp.where(lane == rows - 1, 0.0, pltpu.roll(x, rows - 1, 1))
        return phi(x - below) + phi(x - above) + phi(x - left) + phi(x - right)

    def finish(k, c, before, after):
        x = half[k, c]
        prior = inner(x) + phi(x - before) + phi(x - after)
        share[k, c] = (x - (step_size * prior_weight) * prior).astype(jnp.bfloat16)

    for k in range(2):
        lax.fori_loop(
            1,
            share_cols - 1,
            lambda c, _, k=k: (finish(k, c, half[k, c - 1], half[k, c + 1]), 0)[1],
            0,
        )
    for copy in halo_copies:
        copy.wait()
    has_back = flag((v > 0) | (t > 0))
    has_fore = flag((v < nv - 1) | (t < nt - 1))
    for k in range(2):
        finish(k, 0, halo_in[0, k].astype(jnp.float32) * has_back, half[k, 1])
        finish(
            k,
            share_cols - 1,
            half[k, share_cols - 2],
            halo_in[1, k].astype(jnp.float32) * has_fore,
        )

    up, down, across = view_at(2), view_at(-2), view_at(4)

    def hand_on(source, k, lane, to):
        return remote(
            gathered.at[source, k],
            gathered.at[source, k],
            ag_send.at[lane, k],
            ag_recv.at[lane, k],
            to,
            t,
        )

    other_up, other_down = lax.rem(over + 2, nv), lax.rem(over - 2 + nv, nv)
    other_across = lax.rem(over + 4, nv)
    sent = []

    def go(copy):
        copy.start()
        sent.append(copy)

    def own(k, lane, to):
        return remote(
            share.at[k], gathered.at[v, k], ag_send.at[lane, k], ag_recv.at[lane, k], to, t
        )

    own_copy = pltpu.make_async_copy(share, gathered.at[v], local_sem.at[5 + views])
    for k in range(2):
        go(own(k, 0, up))
        go(own(k, 1, down))
        go(own(k, 2, over))
    own_copy.start()
    for k in range(2):
        if k == 0:
            hand_on(down, 0, 0, up).wait_recv()
            go(hand_on(down, 0, 3, up))
        else:
            hand_on(up, 1, 1, down).wait_recv()
            go(hand_on(up, 1, 3, down))
        hand_on(over, k, 2, over).wait_recv()
        go(hand_on(over, k, 4, up))
        go(hand_on(over, k, 5, down))
    for k in range(2):
        hand_on(across, k, 3, up).wait_recv()
        go(hand_on(across, k, 6, over))
    hand_on(down, 1, 0, up).wait_recv()
    hand_on(up, 0, 1, up).wait_recv()
    for k in range(2):
        hand_on(other_down, k, 4, up).wait_recv()
        hand_on(other_up, k, 5, down).wait_recv()
        hand_on(other_across, k, 6, over).wait_recv()
    for copy in sent:
        copy.wait_send()
    own_copy.wait()


def widen_kernel(object_ref, dual_ref, gathered, object_out, dual_out, volume_out, low, wide, in_sem, out_sem):
    parts, _, share_cols = gathered.shape[:3]

    def load(i):
        return pltpu.make_async_copy(gathered.at[i], low.at[i], in_sem.at[i])

    def store(i):
        return pltpu.make_async_copy(
            wide.at[i], volume_out.at[:, pl.ds(i * share_cols, share_cols)], out_sem.at[i]
        )

    for i in range(parts):
        load(i).start()
    object_out[...] = object_ref[...]
    dual_out[...] = dual_ref[...]

    def step(i, _):
        load(i).wait()
        wide[i] = low[i].astype(jnp.float32)
        store(i).start()
        return 0

    lax.fori_loop(0, parts, step, 0)
    for i in range(parts):
        store(i).wait()


def per_device(
    nv,
    nt,
    object_band,
    dual_band,
    probe_field,
    positions,
    live_counts,
    photon_counts,
    footprints,
    weights,
    volume,
):
    views, _, cols, rows = object_band.shape
    pw = probe_field.shape[1]
    slots = positions.shape[1]
    depth = volume.shape[2]
    share_cols = cols // nv
    span = share_cols * depth
    minus, plus = dft_tables(pw)
    hbm = pl.BlockSpec(memory_space=pltpu.HBM)
    smem = pl.BlockSpec(memory_space=pltpu.SMEM)
    vmem = pl.BlockSpec(memory_space=pltpu.VMEM)
    bf16, f32 = jnp.bfloat16, jnp.float32
    dma = pltpu.SemaphoreType.DMA
    levels = nt // 4
    band = jax.ShapeDtypeStruct(object_band.shape, f32)
    object_new, dual_new, gathered = pl.pallas_call(
        functools.partial(front_kernel, nv, nt),
        out_shape=(
            band,
            band,
            jax.ShapeDtypeStruct((nv, 2, share_cols, depth, rows), bf16),
        ),
        in_specs=[smem] * 3 + [hbm] * 8,
        out_specs=(vmem, vmem, hbm),
        scratch_shapes=[
            pltpu.VMEM(probe_field.shape, f32),
            pltpu.VMEM(minus.shape, bf16),
            pltpu.VMEM(plus.shape, bf16),
            pltpu.VMEM((views, 2, cols, rows), f32),
            pltpu.VMEM((views, 2, 3 * cols, rows), f32),
            pltpu.VMEM((views, slots, pw, rows), jnp.int32),
            pltpu.VMEM(weights.shape, bf16),
            pltpu.VMEM(volume.shape, f32),
            pltpu.VMEM((nv - 1, views, 2 * cols, span), bf16),
            pltpu.VMEM((views * 2 * cols, 2 * rows), f32),
            pltpu.VMEM((levels - 1, 4, views, 2, cols, rows), bf16),
            pltpu.VMEM((levels - 1, 4, views, 2, cols, rows), bf16),
            pltpu.VMEM((3, views, 2, cols, rows), bf16),
            pltpu.VMEM((3, views, 2, cols, rows), bf16),
            pltpu.VMEM((BATCH, 2, 4 * cols, rows), f32),
            pltpu.VMEM((4 * cols, rows), f32),
            pltpu.VMEM((views, 3, 3 * cols, rows), f32),
            pltpu.VMEM((views, 2, 3, cols, rows), bf16),
            pltpu.VMEM((views, 2, 3, cols, rows), bf16),
            pltpu.VMEM((nt, 2, cols, rows), bf16),
            pltpu.VMEM((nt, 2, cols, rows), bf16),
            pltpu.VMEM((nv, 2 * rows, views * 2 * cols), bf16),
            pltpu.VMEM((2 * rows, span), f32),
            pltpu.VMEM((2, share_cols, depth, rows), f32),
            pltpu.VMEM((2, 2, depth, rows), bf16),
            pltpu.VMEM((2, 2, depth, rows), bf16),
            pltpu.VMEM((2, share_cols, depth, rows), bf16),
            dma((6 + views,)),
            dma((2, nv)),
            dma((nv - 1,)),
            dma((nv - 1,)),
            dma((2,)),
            dma((2,)),
            dma((levels - 1,)),
            dma((levels - 1,)),
            dma((3,)),
            dma((3,)),
            dma((views, 2)),
            dma((views, 2)),
            dma((views, 2 * levels)),
            dma((views, 2 * levels)),
            dma((views, 2 * levels)),
            dma((views, 2 * levels)),
            dma((views, nv - 1)),
            dma((views, nv - 1)),
            dma((2,)),
            dma((2,)),
            dma((7, 2)),
            dma((7, 2)),
        ],
        compiler_params=pltpu.CompilerParams(
            collective_id=0, has_side_effects=True, vmem_limit_bytes=FRONT_VMEM * MIB
        ),
        name="front",
    )(
        positions,
        live_counts.reshape(views),
        footprints.reshape(views),
        object_band,
        dual_band,
        probe_field,
        minus,
        plus,
        photon_counts,
        weights,
        volume,
    )
    return pl.pallas_call(
        widen_kernel,
        out_shape=(band, band, jax.ShapeDtypeStruct(volume.shape, f32)),
        in_specs=[vmem, vmem, hbm],
        out_specs=(vmem, vmem, hbm),
        scratch_shapes=[
            pltpu.VMEM(gathered.shape, bf16),
            pltpu.VMEM(gathered.shape, f32),
            dma((nv,)),
            dma((nv,)),
        ],
        compiler_params=pltpu.CompilerParams(vmem_limit_bytes=WIDEN_VMEM * MIB),
        name="widen",
    )(object_new, dual_new, gathered)


def solution(mesh):
    return jax.shard_map(
        functools.partial(per_device, mesh.shape["view"], mesh.shape["tile"]),
        mesh=mesh,
        in_specs=(
            P("view", None, "tile", None),
            P("view", None, "tile", None),
            P(),
            P("view", "tile"),
            P("view", "tile"),
            P("view", "tile", None, None),
            P("view", "tile"),
            P("view", None, "tile"),
            P(None, "tile", None, None),
        ),
        out_specs=(
            P("view", None, "tile", None),
            P("view", None, "tile", None),
            P(None, "tile", None, None),
        ),
        check_vma=False,
    )
```

```python
import functools

import jax
import jax.numpy as jnp
import numpy as np
from jax import lax
from jax.experimental import pallas as pl
from jax.experimental.pallas import tpu as pltpu
from jax.sharding import PartitionSpec as P

rho_weight = 0.5
step_size = 0.5
prior_weight = 0.5
MESH = pl.DeviceIdType.MESH
BATCH = 4
FRONT_VMEM = 60
WIDEN_VMEM = 60
PUMP = (10, 4, 1, 4, 6, 6, 4)
MIB = 2**20


def dft_tables(order):
    counter = np.arange(order)
    angles = ((counter[:, None] * counter[None, :]) % order).astype(np.float32)
    angles = angles * np.float32(2.0 * np.pi / order)
    scaling = np.float32(1.0 / np.sqrt(np.float32(order)))
    re, im = np.cos(angles) * scaling, -np.sin(angles) * scaling
    minus = np.block([[re, -im], [im, re]])
    plus = np.block([[re, im], [-im, re]])
    return jnp.asarray(minus, jnp.bfloat16), jnp.asarray(plus, jnp.bfloat16)


def phi(d):
    return d * lax.rsqrt(1.0 + d * d)


def flag(condition):
    return jnp.where(condition, jnp.float32(1.0), jnp.float32(0.0))


def dot(a, b):
    return jnp.dot(a, b, preferred_element_type=jnp.float32)


def front_kernel(
    nv,
    nt,
    positions,
    live_counts,
    footprints,
    object_hbm,
    dual_hbm,
    probe_hbm,
    minus_hbm,
    plus_hbm,
    counts_hbm,
    weights_hbm,
    volume_hbm,
    object_out,
    dual_out,
    gathered,
    probe,
    minus,
    plus,
    dual_v,
    reach,
    counts_v,
    weights_v,
    volume_v,
    weights_in,
    shadow,
    shadow_out,
    shadow_in,
    shared_out,
    shared_in,
    patch_tmp,
    power_tmp,
    acc,
    upd_out,
    upd_in,
    resid_first,
    resid_second,
    rt,
    grad,
    half,
    halo_out,
    halo_in,
    share,
    local_sem,
    chunk_sem,
    w_send,
    w_recv,
    obj_send,
    obj_recv,
    sh_send,
    sh_recv,
    gr_send,
    gr_recv,
    upd_send,
    upd_recv,
    res_send,
    res_recv,
    rel_send,
    rel_recv,
    rt_send,
    rt_recv,
    halo_send,
    halo_recv,
    ag_send,
    ag_recv,
):
    v = lax.axis_index("view")
    t = lax.axis_index("tile")
    views, slots = positions.shape
    resid_full = (resid_first, resid_second)
    cols = reach.shape[2] // 3
    depth = volume_hbm.shape[2]
    share_cols = cols // nv
    span = share_cols * depth
    rows = probe.shape[2]
    pw = probe.shape[1]

    def remote(src, dst, send, recv, view, tile):
        return pltpu.make_async_remote_copy(
            src_ref=src,
            dst_ref=dst,
            send_sem=send,
            recv_sem=recv,
            device_id={"view": view, "tile": tile},
            device_id_type=MESH,
        )

    def view_at(k):
        return lax.rem(v + k + nv, nv)

    def tile_at(k):
        return lax.rem(t + k + nt, nt)

    group = 4
    levels = nt // group
    z, place = t // group, lax.rem(t, group)
    core = lax.rem(t, 2)
    sibling = t + 1 - 2 * core
    beside = t + 2 - 4 * (place // 2)
    view_x = lax.rem(v, 2)
    over = v + 1 - 2 * view_x

    def level_at(k):
        return lax.rem(z + k + levels, levels)

    back_v, back_t = view_at(-1), jnp.where(v == 0, tile_at(-1), t)
    fore_v, fore_t = view_at(1), jnp.where(v == nv - 1, tile_at(1), t)

    loads = [
        pltpu.make_async_copy(object_hbm, reach.at[:, :, pl.ds(0, cols), :], local_sem.at[0]),
        pltpu.make_async_copy(dual_hbm, dual_v, local_sem.at[1]),
    ]
    for a in range(views):
        loads.append(
            pltpu.make_async_copy(counts_hbm.at[a], counts_v.at[a], local_sem.at[2 + a])
        )
    for i, (source, target) in enumerate(
        ((probe_hbm, probe), (minus_hbm, minus), (plus_hbm, plus))
    ):
        loads.append(pltpu.make_async_copy(source, target, local_sem.at[2 + views + i]))

    def chunk_copies(c):
        first = pl.multiple_of(c * span, span)
        return (
            pltpu.make_async_copy(
                weights_hbm.at[:, :, pl.ds(first, span)],
                weights_v.at[:, :, pl.ds(first, span)],
                chunk_sem.at[0, c],
            ),
            pltpu.make_async_copy(
                volume_hbm.at[:, pl.ds(c * share_cols, share_cols)],
                volume_v.at[:, pl.ds(c * share_cols, share_cols)],
                chunk_sem.at[1, c],
            ),
        )

    loads[0].start()
    for c in range(nv):
        for copy in chunk_copies(c):
            copy.start()
    for copy in loads[1:]:
        copy.start()

    barrier = pltpu.get_barrier_semaphore()

    def greet(view, tile):
        pl.semaphore_signal(
            barrier, inc=1, device_id={"view": view, "tile": tile}, device_id_type=MESH
        )

    for k in range(1, nv):
        greet(view_at(k), t)
    for k in range(1, nt):
        greet(v, tile_at(k))
    greet(back_v, back_t)
    greet(fore_v, fore_t)
    pl.semaphore_wait(barrier, nv + nt)

    object_copies = [
        remote(
            object_hbm,
            reach.at[:, :, pl.ds(k * cols, cols), :],
            obj_send.at[k - 1],
            obj_recv.at[k - 1],
            v,
            tile_at(-k),
        )
        for k in (1, 2)
    ]
    for copy in object_copies:
        copy.start()

    peers = nv - 1
    piece_rows = 32
    per_view = 2 * cols // piece_rows
    pieces = peers * views * per_view

    def pump(first, count):
        for extra in range(count):
            index = first + extra
            k = index % peers
            row_block = index // peers
            a = row_block // per_view
            rows_at = pl.multiple_of((row_block % per_view) * piece_rows, piece_rows)
            lane = k + 1
            to = lax.rem(v - view_x + 2 * (lane // 2), nv) + lax.rem(view_x + lane, 2)
            remote(
                weights_hbm.at[a, pl.ds(rows_at, piece_rows), pl.ds(pl.multiple_of(to * span, span), span)],
                weights_in.at[k, a, pl.ds(rows_at, piece_rows), :],
                w_send.at[k],
                w_recv.at[k],
                to,
                t,
            ).start()

    pumped = 0

    def pump_some(count):
        nonlocal pumped
        count = min(count, pieces - pumped)
        pump(pumped, count)
        pumped += count

    pump_some(PUMP[0])

    shadow[...] = jnp.zeros_like(shadow)

    def project(c, _):
        for copy in chunk_copies(c):
            copy.wait()
        first = pl.multiple_of(c * span, span)
        left = weights_v[:, :, pl.ds(first, span)].reshape(views * 2 * cols, span)
        block = volume_v[:, pl.ds(c * share_cols, share_cols)].astype(jnp.bfloat16)
        right = jnp.concatenate(
            [block[0].reshape(span, rows), block[1].reshape(span, rows)], axis=1
        )
        shadow[...] += dot(left, right)
        return 0

    lax.fori_loop(0, nv, project, 0)

    foot = [footprints[a] for a in range(views)]

    def shadow_part(a, k, part):
        first = a * 2 * cols + part * cols
        return shadow[first : first + cols, k * rows : (k + 1) * rows]

    def placed(to, a, k):
        return shadow_part(a, k, 0) * flag(foot[a] == to) + shadow_part(a, k, 1) * flag(
            foot[a] + 1 == to
        )

    def level_copy(k, a):
        return remote(
            shadow_out.at[k - 1, a],
            shadow_in.at[k - 1, a],
            sh_send.at[k - 1, a],
            sh_recv.at[k - 1, a],
            v,
            level_at(k) * group + place,
        )

    def group_copy(k, a):
        return remote(
            shared_out.at[k - 1, a],
            shared_in.at[k - 1, a],
            gr_send.at[k - 1, a],
            gr_recv.at[k - 1, a],
            v,
            z * group + lax.rem(place + k, group),
        )

    for a in range(views):
        for step in range(1, levels):
            for k in range(group):
                to = level_at(step) * group + k
                for plane in range(2):
                    shadow_out[step - 1, a, k, plane] = placed(to, a, plane).astype(jnp.bfloat16)
            level_copy(step, a).start()

    def level_sum(to, k, a, plane):
        total = placed(to, a, plane)
        for step in range(1, levels):
            total = total + shadow_in[step - 1, a, k, plane].astype(jnp.float32)
        return total

    def share_sums(a):
        for step in range(1, levels):
            level_copy(step, a).wait()
        for step in range(1, group):
            k = lax.rem(place + step, group)
            for plane in range(2):
                shared_out[step - 1, a, plane] = level_sum(z * group + k, k, a, plane).astype(
                    jnp.bfloat16
                )
            group_copy(step, a).start()

    pump_some(PUMP[1])

    for copy in loads[2 + views :]:
        copy.wait()
    probe_re, probe_im = probe[0], probe[1]
    acc[...] = jnp.zeros_like(acc)
    patch_tmp[...] = jnp.zeros_like(patch_tmp)
    power_tmp[...] = jnp.zeros_like(power_tmp)
    power_tmp[cols : cols + pw, :] = probe_re * probe_re + probe_im * probe_im
    for copy in loads[:2]:
        copy.wait()
    for copy in object_copies:
        copy.wait()
    for k in (1, 2):
        inside = flag(t + k < nt)
        for a in range(views):
            for plane in range(2):
                reach[a, plane, k * cols : (k + 1) * cols, :] = (
                    reach[a, plane, k * cols : (k + 1) * cols, :] * inside
                )

    def patches(a, b):
        base = b * BATCH
        offsets = [positions[a, base + j] for j in range(BATCH)]
        live_count = live_counts[a]
        lives = [flag(base + j < live_count) for j in range(BATCH)]
        re, im = probe[0], probe[1]
        exits = []
        for j in range(BATCH):
            obj_re = reach[a, 0, pl.ds(offsets[j], pw), :]
            obj_im = reach[a, 1, pl.ds(offsets[j], pw), :]
            exits.append(
                jnp.concatenate(
                    [re * obj_re - im * obj_im, re * obj_im + im * obj_re], axis=0
                ).astype(jnp.bfloat16)
            )
        done = dot(minus[...], jnp.concatenate(exits, axis=1)).astype(jnp.bfloat16)
        done = jnp.concatenate(
            [
                jnp.concatenate(
                    [
                        done[:pw, j * rows : (j + 1) * rows],
                        done[pw:, j * rows : (j + 1) * rows],
                    ],
                    axis=1,
                )
                for j in range(BATCH)
            ],
            axis=0,
        )
        spectrum = dot(done, plus[...])
        s_re, s_im = spectrum[:, :rows], spectrum[:, rows:]
        counts = counts_v[a, pl.ds(base, BATCH)].astype(jnp.float32).reshape(BATCH * pw, rows)
        power = 256.0 * (s_re * s_re + s_im * s_im) + 64.0
        factor = counts * lax.rsqrt(jnp.maximum(counts * power, 1e-20))
        replaced = jnp.concatenate([s_re * factor, s_im * factor], axis=1).astype(jnp.bfloat16)
        inverse = dot(replaced, minus[...]).astype(jnp.bfloat16)
        inverse = jnp.concatenate(
            [
                jnp.concatenate(
                    [
                        inverse[j * pw : (j + 1) * pw, :rows],
                        inverse[j * pw : (j + 1) * pw, rows:],
                    ],
                    axis=0,
                )
                for j in range(BATCH)
            ],
            axis=1,
        )
        wave = dot(plus[...], inverse)
        for j in range(BATCH):
            diff = wave[:, j * rows : (j + 1) * rows] - exits[j].astype(jnp.float32)
            d_re, d_im = diff[:pw] * lives[j], diff[pw:] * lives[j]
            patch_tmp[j, 0, cols : cols + pw, :] = re * d_re + im * d_im
            patch_tmp[j, 1, cols : cols + pw, :] = re * d_im - im * d_re
        for plane in range(2):
            total = acc[a, plane]
            for j in range(BATCH):
                total = total + patch_tmp[j, plane, pl.ds(cols - offsets[j], 3 * cols), :]
            acc[a, plane] = total
        total = acc[a, 2]
        for j in range(BATCH):
            total = total + power_tmp[pl.ds(cols - offsets[j], 3 * cols), :] * lives[j]
        acc[a, 2] = total

    def update_copy(a, k):
        return remote(
            upd_out.at[a, k - 1],
            upd_in.at[a, k - 1],
            upd_send.at[a, k - 1],
            upd_recv.at[a, k - 1],
            v,
            tile_at(k),
        )

    def run_patches(a, first, last):
        nonlocal pumped
        each = min(PUMP[2], (pieces - pumped) // (last - first))
        base = pumped

        def body(b, _):
            pump(base + (b - first) * each, each)
            patches(a, b)
            return 0

        lax.fori_loop(first, last, body, 0)
        pumped += each * (last - first)

    def send_update(a):
        for k in (1, 2):
            upd_out[a, k - 1] = acc[a, :, k * cols : (k + 1) * cols, :].astype(jnp.bfloat16)
            update_copy(a, k).start()

    from_one, from_two = flag(t >= 1), flag(t >= 2)

    def finish_object(a):
        for step in range(1, group):
            group_copy(step, a).wait()
        for k in (1, 2):
            update_copy(a, k).wait()
        upd = (
            acc[a, :, :cols, :]
            + upd_in[a, 0].astype(jnp.float32) * from_one
            + upd_in[a, 1].astype(jnp.float32) * from_two
        )
        scale = 1.0 / (1.0 + upd[2])
        for k in range(2):
            projection = level_sum(t, place, a, k)
            for step in range(1, group):
                projection = projection + shared_in[step - 1, a, k].astype(jnp.float32)
            obj = reach[a, k, :cols, :]
            dual = dual_v[a, k]
            new = obj + upd[k] * scale - rho_weight * (obj - projection - dual)
            object_out[a, k] = new
            dual_new = dual + projection - new
            dual_out[a, k] = dual_new
            resid_full[a][t, k] = dual_new.astype(jnp.bfloat16)

    def source_at(lane, tile):
        k, j = lane // 2, lane % 2
        base = lax.rem(tile // group - k + levels, levels) * group
        spot = lax.rem(tile, group)
        return base + (lax.rem(spot + 2, group) if j else spot)

    lanes = 2 * levels

    def resid_copy(a, lane, source, to):
        return remote(
            resid_full[a].at[source],
            resid_full[a].at[source],
            res_send.at[a, lane],
            res_recv.at[a, lane],
            v,
            to,
        )

    def relay_copy(a, lane, source):
        return remote(
            resid_full[a].at[source],
            resid_full[a].at[source],
            rel_send.at[a, lane],
            rel_recv.at[a, lane],
            v,
            sibling,
        )

    def send_resid(a):
        resid_copy(a, 1, t, beside).start()
        for k in range(1, levels):
            resid_copy(a, 2 * k, t, level_at(k) * group + place).start()
        relay_copy(a, 0, t).start()

    def relay_resid(a):
        resid_copy(a, 1, beside, beside).wait_recv()
        for k in range(1, levels):
            resid_copy(a, 2 * k + 1, beside, level_at(k) * group + place).start()
        relay_copy(a, 1, beside).start()
        for lane in range(2, lanes):
            source = source_at(lane, t)
            resid_copy(a, lane, source, t).wait_recv()
            relay_copy(a, lane, source).start()

    def rt_part(k, a):
        return rt.at[k, :, pl.ds(a * 2 * cols, 2 * cols)]

    def rt_copy(a, lane, k, to):
        return remote(
            rt_part(k, a),
            rt_part(lane, a),
            rt_send.at[a, lane - 1],
            rt_recv.at[a, lane - 1],
            to,
            t,
        )

    def spread_windows(a):
        rt_copy(a, 1, 1, over).wait_recv()
        for k in range(1, nv // 2):
            rt_copy(a, 2 * k + 1, 1, view_at(2 * k)).start()

    def send_windows(a):
        for lane in range(lanes):
            relay_copy(a, lane, source_at(lane, sibling)).wait_recv()
            relay_copy(a, lane, source_at(lane, t)).wait_send()
        for lane in range(1, lanes):
            resid_copy(a, lane, t, t).wait_send()
        for k in range(2):
            window = jnp.concatenate(
                [resid_full[a][foot[a], k], resid_full[a][foot[a] + 1, k]], axis=0
            )
            rt[0, k * rows : (k + 1) * rows, a * 2 * cols : (a + 1) * 2 * cols] = (
                window.astype(jnp.float32).T.astype(jnp.bfloat16)
            )
        rt_copy(a, 1, 0, over).start()
        for k in range(1, nv // 2):
            rt_copy(a, 2 * k, 0, view_at(2 * k)).start()

    batches = slots // BATCH
    for a in range(views):
        loads[2 + a].wait()
        run_patches(a, 0, batches)
        send_update(a)
        share_sums(a)
    pump_some(PUMP[3])
    for a in range(views):
        finish_object(a)
        send_resid(a)
    pump_some(PUMP[4])
    for a in range(views):
        relay_resid(a)
    pump_some(PUMP[5])
    for a in range(views):
        send_windows(a)
    pump_some(PUMP[6])
    for a in range(views):
        spread_windows(a)
    pump_some(pieces)

    own = weights_v[:, :, pl.ds(pl.multiple_of(v * span, span), span)]
    grad[...] = dot(rt[0], own.reshape(views * 2 * cols, span))
    for lane in (1, *range(2, nv, 2), *range(3, nv, 2)):
        for a in range(views):
            if lane > 1:
                rt_copy(a, lane, 0, v).wait_recv()
            rt_copy(a, lane, 0, v).wait_send()
        k = lane
        remote(
            weights_hbm.at[:, :, pl.ds(0, span)],
            weights_in.at[k - 1],
            w_send.at[k - 1],
            w_recv.at[k - 1],
            view_at(k),
            t,
        ).wait()
        grad[...] += dot(rt[lane], weights_in[k - 1].reshape(views * 2 * cols, span))

    for c in range(share_cols):
        for k in range(2):
            part = grad[k * rows : (k + 1) * rows, c * depth : (c + 1) * depth].T
            half[k, c] = volume_v[k, v * share_cols + c] - step_size * part

    for k in range(2):
        halo_out[0, k] = half[k, 0].astype(jnp.bfloat16)
        halo_out[1, k] = half[k, share_cols - 1].astype(jnp.bfloat16)
    halo_copies = [
        remote(halo_out.at[0], halo_in.at[1], halo_send.at[0], halo_recv.at[1], back_v, back_t),
        remote(halo_out.at[1], halo_in.at[0], halo_send.at[1], halo_recv.at[0], fore_v, fore_t),
    ]
    for copy in halo_copies:
        copy.start()

    row = lax.broadcasted_iota(jnp.int32, (depth, rows), 0)
    lane = lax.broadcasted_iota(jnp.int32, (depth, rows), 1)

    def inner(x):
        below = jnp.where(row == 0, 0.0, pltpu.roll(x, 1, 0))
        above = jnp.where(row == depth - 1, 0.0, pltpu.roll(x, depth - 1, 0))
        left = jnp.where(lane == 0, 0.0, pltpu.roll(x, 1, 1))
        right = jnp.where(lane == rows - 1, 0.0, pltpu.roll(x, rows - 1, 1))
        return phi(x - below) + phi(x - above) + phi(x - left) + phi(x - right)

    def finish(k, c, slot, before, after):
        x = half[k, c]
        prior = inner(x) + phi(x - before) + phi(x - after)
        share[k, slot] = (x - (step_size * prior_weight) * prior).astype(jnp.bfloat16)

    up, down, across = view_at(2), view_at(-2), view_at(4)
    other_up, other_down = lax.rem(over + 2, nv), lax.rem(over - 2 + nv, nv)
    other_across = lax.rem(over + 4, nv)
    inner_cols = share_cols - 2
    spans = (pl.ds(0, inner_cols), pl.ds(inner_cols, 2))
    sent = []

    def go(copy):
        copy.start()
        sent.append(copy)

    def hand_on(source, k, part, lane, to):
        return remote(
            gathered.at[source, k, spans[part]],
            gathered.at[source, k, spans[part]],
            ag_send.at[lane, k, part],
            ag_recv.at[lane, k, part],
            to,
            t,
        )

    def own(k, part, lane, to):
        return remote(
            share.at[k, spans[part]],
            gathered.at[v, k, spans[part]],
            ag_send.at[lane, k, part],
            ag_recv.at[lane, k, part],
            to,
            t,
        )

    def send_own(k, part):
        go(own(k, part, 0, up))
        go(own(k, part, 1, down))
        go(own(k, part, 2, over))

    for k in range(2):
        lax.fori_loop(
            1,
            share_cols - 1,
            lambda c, _, k=k: (finish(k, c, c - 1, half[k, c - 1], half[k, c + 1]), 0)[1],
            0,
        )
        send_own(k, 0)
    for copy in halo_copies:
        copy.wait()
    has_back = flag((v > 0) | (t > 0))
    has_fore = flag((v < nv - 1) | (t < nt - 1))
    for k in range(2):
        finish(k, 0, share_cols - 2, halo_in[0, k].astype(jnp.float32) * has_back, half[k, 1])
        finish(
            k,
            share_cols - 1,
            share_cols - 1,
            half[k, share_cols - 2],
            halo_in[1, k].astype(jnp.float32) * has_fore,
        )
        send_own(k, 1)

    own_copy = pltpu.make_async_copy(share, gathered.at[v], local_sem.at[5 + views])
    own_copy.start()
    for part in range(2):
        for k in range(2):
            if k == 0:
                hand_on(down, 0, part, 0, up).wait_recv()
                go(hand_on(down, 0, part, 3, up))
            else:
                hand_on(up, 1, part, 1, down).wait_recv()
                go(hand_on(up, 1, part, 3, down))
            hand_on(over, k, part, 2, over).wait_recv()
            go(hand_on(over, k, part, 4, up))
            go(hand_on(over, k, part, 5, down))
    for part in range(2):
        for k in range(2):
            hand_on(across, k, part, 3, up).wait_recv()
            go(hand_on(across, k, part, 6, over))
    for part in range(2):
        hand_on(down, 1, part, 0, up).wait_recv()
        hand_on(up, 0, part, 1, up).wait_recv()
        for k in range(2):
            hand_on(other_down, k, part, 4, up).wait_recv()
            hand_on(other_up, k, part, 5, down).wait_recv()
            hand_on(other_across, k, part, 6, over).wait_recv()
    for copy in sent:
        copy.wait_send()
    own_copy.wait()


def widen_kernel(object_ref, dual_ref, gathered, object_out, dual_out, volume_out, low, wide, in_sem, out_sem):
    parts, _, share_cols = gathered.shape[:3]

    def load(i):
        return pltpu.make_async_copy(gathered.at[i], low.at[i], in_sem.at[i])

    def store(i):
        return pltpu.make_async_copy(
            wide.at[i], volume_out.at[:, pl.ds(i * share_cols, share_cols)], out_sem.at[i]
        )

    for i in range(parts):
        load(i).start()
    object_out[...] = object_ref[...]
    dual_out[...] = dual_ref[...]

    def step(i, _):
        load(i).wait()
        wide[i, :, 1 : share_cols - 1] = low[i, :, : share_cols - 2].astype(jnp.float32)
        wide[i, :, 0] = low[i, :, share_cols - 2].astype(jnp.float32)
        wide[i, :, share_cols - 1] = low[i, :, share_cols - 1].astype(jnp.float32)
        store(i).start()
        return 0

    lax.fori_loop(0, parts, step, 0)
    for i in range(parts):
        store(i).wait()


def per_device(
    nv,
    nt,
    object_band,
    dual_band,
    probe_field,
    positions,
    live_counts,
    photon_counts,
    footprints,
    weights,
    volume,
):
    views, _, cols, rows = object_band.shape
    pw = probe_field.shape[1]
    slots = positions.shape[1]
    depth = volume.shape[2]
    share_cols = cols // nv
    span = share_cols * depth
    minus, plus = dft_tables(pw)
    hbm = pl.BlockSpec(memory_space=pltpu.HBM)
    smem = pl.BlockSpec(memory_space=pltpu.SMEM)
    vmem = pl.BlockSpec(memory_space=pltpu.VMEM)
    bf16, f32 = jnp.bfloat16, jnp.float32
    dma = pltpu.SemaphoreType.DMA
    levels = nt // 4
    band = jax.ShapeDtypeStruct(object_band.shape, f32)
    object_new, dual_new, gathered = pl.pallas_call(
        functools.partial(front_kernel, nv, nt),
        out_shape=(
            band,
            band,
            jax.ShapeDtypeStruct((nv, 2, share_cols, depth, rows), bf16),
        ),
        in_specs=[smem] * 3 + [hbm] * 8,
        out_specs=(vmem, vmem, hbm),
        scratch_shapes=[
            pltpu.VMEM(probe_field.shape, f32),
            pltpu.VMEM(minus.shape, bf16),
            pltpu.VMEM(plus.shape, bf16),
            pltpu.VMEM((views, 2, cols, rows), f32),
            pltpu.VMEM((views, 2, 3 * cols, rows), f32),
            pltpu.VMEM((views, slots, pw, rows), jnp.int32),
            pltpu.VMEM(weights.shape, bf16),
            pltpu.VMEM(volume.shape, f32),
            pltpu.VMEM((nv - 1, views, 2 * cols, span), bf16),
            pltpu.VMEM((views * 2 * cols, 2 * rows), f32),
            pltpu.VMEM((levels - 1, views, 4, 2, cols, rows), bf16),
            pltpu.VMEM((levels - 1, views, 4, 2, cols, rows), bf16),
            pltpu.VMEM((3, views, 2, cols, rows), bf16),
            pltpu.VMEM((3, views, 2, cols, rows), bf16),
            pltpu.VMEM((BATCH, 2, 4 * cols, rows), f32),
            pltpu.VMEM((4 * cols, rows), f32),
            pltpu.VMEM((views, 3, 3 * cols, rows), f32),
            pltpu.VMEM((views, 2, 3, cols, rows), bf16),
            pltpu.VMEM((views, 2, 3, cols, rows), bf16),
            pltpu.VMEM((nt, 2, cols, rows), bf16),
            pltpu.VMEM((nt, 2, cols, rows), bf16),
            pltpu.VMEM((nv, 2 * rows, views * 2 * cols), bf16),
            pltpu.VMEM((2 * rows, span), f32),
            pltpu.VMEM((2, share_cols, depth, rows), f32),
            pltpu.VMEM((2, 2, depth, rows), bf16),
            pltpu.VMEM((2, 2, depth, rows), bf16),
            pltpu.VMEM((2, share_cols, depth, rows), bf16),
            dma((6 + views,)),
            dma((2, nv)),
            dma((nv - 1,)),
            dma((nv - 1,)),
            dma((2,)),
            dma((2,)),
            dma((levels - 1, views)),
            dma((levels - 1, views)),
            dma((3, views)),
            dma((3, views)),
            dma((views, 2)),
            dma((views, 2)),
            dma((views, 2 * levels)),
            dma((views, 2 * levels)),
            dma((views, 2 * levels)),
            dma((views, 2 * levels)),
            dma((views, nv - 1)),
            dma((views, nv - 1)),
            dma((2,)),
            dma((2,)),
            dma((7, 2, 2)),
            dma((7, 2, 2)),
        ],
        compiler_params=pltpu.CompilerParams(
            collective_id=0, has_side_effects=True, vmem_limit_bytes=FRONT_VMEM * MIB
        ),
        name="front",
    )(
        positions,
        live_counts.reshape(views),
        footprints.reshape(views),
        object_band,
        dual_band,
        probe_field,
        minus,
        plus,
        photon_counts,
        weights,
        volume,
    )
    return pl.pallas_call(
        widen_kernel,
        out_shape=(band, band, jax.ShapeDtypeStruct(volume.shape, f32)),
        in_specs=[vmem, vmem, hbm],
        out_specs=(vmem, vmem, hbm),
        scratch_shapes=[
            pltpu.VMEM(gathered.shape, bf16),
            pltpu.VMEM(gathered.shape, f32),
            dma((nv,)),
            dma((nv,)),
        ],
        compiler_params=pltpu.CompilerParams(vmem_limit_bytes=WIDEN_VMEM * MIB),
        name="widen",
    )(object_new, dual_new, gathered)


def solution(mesh):
    return jax.shard_map(
        functools.partial(per_device, mesh.shape["view"], mesh.shape["tile"]),
        mesh=mesh,
        in_specs=(
            P("view", None, "tile", None),
            P("view", None, "tile", None),
            P(),
            P("view", "tile"),
            P("view", "tile"),
            P("view", "tile", None, None),
            P("view", "tile"),
            P("view", None, "tile"),
            P(None, "tile", None, None),
        ),
        out_specs=(
            P("view", None, "tile", None),
            P("view", None, "tile", None),
            P(None, "tile", None, None),
        ),
        check_vma=False,
    )
```

```python
import functools

import jax
import jax.numpy as jnp
import numpy as np
from jax import lax
from jax.experimental import pallas as pl
from jax.experimental.pallas import tpu as pltpu
from jax.sharding import PartitionSpec as P

rho_weight = 0.5
step_size = 0.5
prior_weight = 0.5
MESH = pl.DeviceIdType.MESH
BATCH = 4
PIECE_ROWS = 16
FRONT_VMEM = 60
WIDEN_VMEM = 60
PUMP = (16, 6, 1, 2, 4, 4)
MIB = 2**20


def dft_tables(order):
    counter = np.arange(order)
    angles = ((counter[:, None] * counter[None, :]) % order).astype(np.float32)
    angles = angles * np.float32(2.0 * np.pi / order)
    scaling = np.float32(1.0 / np.sqrt(np.float32(order)))
    re, im = np.cos(angles) * scaling, -np.sin(angles) * scaling
    minus = np.block([[re, -im], [im, re]])
    plus = np.block([[re, im], [-im, re]])
    return jnp.asarray(minus, jnp.bfloat16), jnp.asarray(plus, jnp.bfloat16)


def phi(d):
    return d * lax.rsqrt(1.0 + d * d)


def flag(condition):
    return jnp.where(condition, jnp.float32(1.0), jnp.float32(0.0))


def dot(a, b):
    return jnp.dot(a, b, preferred_element_type=jnp.float32)


def front_kernel(
    nv,
    nt,
    positions,
    live_counts,
    footprints,
    object_hbm,
    dual_hbm,
    probe_hbm,
    minus_hbm,
    plus_hbm,
    counts_hbm,
    weights_hbm,
    volume_hbm,
    object_out,
    dual_out,
    gathered,
    probe,
    minus,
    plus,
    dual_v,
    reach,
    counts_v,
    weights_v,
    volume_v,
    weights_in,
    shadow,
    shadow_out,
    shadow_in,
    shared_out,
    shared_in,
    patch_tmp,
    power_tmp,
    acc,
    upd_out,
    upd_in,
    resid_first,
    resid_second,
    rt,
    grad,
    pair_out,
    pair_in,
    half,
    halo_out,
    halo_in,
    share,
    local_sem,
    chunk_sem,
    w_send,
    w_recv,
    obj_send,
    obj_recv,
    sh_send,
    sh_recv,
    gr_send,
    gr_recv,
    upd_send,
    upd_recv,
    res_send,
    res_recv,
    rel_send,
    rel_recv,
    rt_send,
    rt_recv,
    pair_send,
    pair_recv,
    halo_send,
    halo_recv,
    ag_send,
    ag_recv,
):
    v = lax.axis_index("view")
    t = lax.axis_index("tile")
    views, slots = positions.shape
    resid_full = (resid_first, resid_second)
    cols = reach.shape[2] // 3
    depth = volume_hbm.shape[2]
    share_cols = cols // nv
    span = share_cols * depth
    rows = probe.shape[2]
    pw = probe.shape[1]

    def remote(src, dst, send, recv, view, tile):
        return pltpu.make_async_remote_copy(
            src_ref=src,
            dst_ref=dst,
            send_sem=send,
            recv_sem=recv,
            device_id={"view": view, "tile": tile},
            device_id_type=MESH,
        )

    def view_at(k):
        return lax.rem(v + k + nv, nv)

    def tile_at(k):
        return lax.rem(t + k + nt, nt)

    group = 4
    levels = nt // group
    z, place = t // group, lax.rem(t, group)
    core = lax.rem(t, 2)
    sibling = t + 1 - 2 * core
    beside = t + 2 - 4 * (place // 2)
    view_x = lax.rem(v, 2)
    over = v + 1 - 2 * view_x

    def level_at(k):
        return lax.rem(z + k + levels, levels)

    back_v, back_t = view_at(-1), jnp.where(v == 0, tile_at(-1), t)
    fore_v, fore_t = view_at(1), jnp.where(v == nv - 1, tile_at(1), t)

    loads = [
        pltpu.make_async_copy(object_hbm, reach.at[:, :, pl.ds(0, cols), :], local_sem.at[0]),
        pltpu.make_async_copy(dual_hbm, dual_v, local_sem.at[1]),
    ]
    for a in range(views):
        loads.append(
            pltpu.make_async_copy(counts_hbm.at[a], counts_v.at[a], local_sem.at[2 + a])
        )
    for i, (source, target) in enumerate(
        ((probe_hbm, probe), (minus_hbm, minus), (plus_hbm, plus))
    ):
        loads.append(pltpu.make_async_copy(source, target, local_sem.at[2 + views + i]))

    def chunk_copies(c):
        first = pl.multiple_of(c * span, span)
        return (
            pltpu.make_async_copy(
                weights_hbm.at[:, :, pl.ds(first, span)],
                weights_v.at[:, :, pl.ds(first, span)],
                chunk_sem.at[0, c],
            ),
            pltpu.make_async_copy(
                volume_hbm.at[:, pl.ds(c * share_cols, share_cols)],
                volume_v.at[:, pl.ds(c * share_cols, share_cols)],
                chunk_sem.at[1, c],
            ),
        )

    loads[0].start()
    for c in range(nv):
        for copy in chunk_copies(c):
            copy.start()
    for copy in loads[1:]:
        copy.start()

    barrier = pltpu.get_barrier_semaphore()

    def greet(view, tile):
        pl.semaphore_signal(
            barrier, inc=1, device_id={"view": view, "tile": tile}, device_id_type=MESH
        )

    for k in range(1, nv):
        greet(view_at(k), t)
    for k in range(1, nt):
        greet(v, tile_at(k))
    greet(back_v, back_t)
    greet(fore_v, fore_t)
    pl.semaphore_wait(barrier, nv + nt)

    object_copies = [
        remote(
            object_hbm,
            reach.at[:, :, pl.ds(k * cols, cols), :],
            obj_send.at[k - 1],
            obj_recv.at[k - 1],
            v,
            tile_at(-k),
        )
        for k in (1, 2)
    ]
    for copy in object_copies:
        copy.start()

    peers = nv // 2 - 1
    piece_rows = PIECE_ROWS
    wide_span = 2 * span
    per_view = 2 * cols // piece_rows
    pieces = peers * views * per_view

    def pump(first, count):
        for extra in range(count):
            index = first + extra
            k = index % peers
            row_block = index // peers
            a = row_block // per_view
            rows_at = pl.multiple_of((row_block % per_view) * piece_rows, piece_rows)
            to = lax.rem(v + 2 * (k + 1), nv)
            first_voxel = pl.multiple_of((to // 2) * wide_span, wide_span)
            remote(
                weights_hbm.at[a, pl.ds(rows_at, piece_rows), pl.ds(first_voxel, wide_span)],
                weights_in.at[k, a, pl.ds(rows_at, piece_rows), :],
                w_send.at[k],
                w_recv.at[k],
                to,
                t,
            ).start()

    pumped = 0

    def pump_some(count):
        nonlocal pumped
        count = min(count, pieces - pumped)
        pump(pumped, count)
        pumped += count

    pump_some(PUMP[0])

    shadow[...] = jnp.zeros_like(shadow)

    def project(c, _):
        for copy in chunk_copies(c):
            copy.wait()
        first = pl.multiple_of(c * span, span)
        left = weights_v[:, :, pl.ds(first, span)].reshape(views * 2 * cols, span)
        block = volume_v[:, pl.ds(c * share_cols, share_cols)].astype(jnp.bfloat16)
        right = jnp.concatenate(
            [block[0].reshape(span, rows), block[1].reshape(span, rows)], axis=1
        )
        shadow[...] += dot(left, right)
        return 0

    lax.fori_loop(0, nv, project, 0)

    foot = [footprints[a] for a in range(views)]

    def shadow_part(a, k, part):
        first = a * 2 * cols + part * cols
        return shadow[first : first + cols, k * rows : (k + 1) * rows]

    def placed(to, a, k):
        return shadow_part(a, k, 0) * flag(foot[a] == to) + shadow_part(a, k, 1) * flag(
            foot[a] + 1 == to
        )

    def level_copy(k, a):
        return remote(
            shadow_out.at[k - 1, a],
            shadow_in.at[k - 1, a],
            sh_send.at[k - 1, a],
            sh_recv.at[k - 1, a],
            v,
            level_at(k) * group + place,
        )

    def group_copy(k, a):
        return remote(
            shared_out.at[k - 1, a],
            shared_in.at[k - 1, a],
            gr_send.at[k - 1, a],
            gr_recv.at[k - 1, a],
            v,
            z * group + lax.rem(place + k, group),
        )

    for a in range(views):
        for step in range(1, levels):
            for k in range(group):
                to = level_at(step) * group + k
                for plane in range(2):
                    shadow_out[step - 1, a, k, plane] = placed(to, a, plane).astype(jnp.bfloat16)
            level_copy(step, a).start()

    def level_sum(to, k, a, plane):
        total = placed(to, a, plane)
        for step in range(1, levels):
            total = total + shadow_in[step - 1, a, k, plane].astype(jnp.float32)
        return total

    def share_sums(a):
        for step in range(1, levels):
            level_copy(step, a).wait()
        for step in range(1, group):
            k = lax.rem(place + step, group)
            for plane in range(2):
                shared_out[step - 1, a, plane] = level_sum(z * group + k, k, a, plane).astype(
                    jnp.bfloat16
                )
            group_copy(step, a).start()

    pump_some(PUMP[1])

    for copy in loads[2 + views :]:
        copy.wait()
    probe_re, probe_im = probe[0], probe[1]
    acc[...] = jnp.zeros_like(acc)
    patch_tmp[...] = jnp.zeros_like(patch_tmp)
    power_tmp[...] = jnp.zeros_like(power_tmp)
    power_tmp[cols : cols + pw, :] = probe_re * probe_re + probe_im * probe_im
    for copy in loads[:2]:
        copy.wait()
    for copy in object_copies:
        copy.wait()
    for k in (1, 2):
        inside = flag(t + k < nt)
        for a in range(views):
            for plane in range(2):
                reach[a, plane, k * cols : (k + 1) * cols, :] = (
                    reach[a, plane, k * cols : (k + 1) * cols, :] * inside
                )

    def patches(a, b):
        base = b * BATCH
        offsets = [positions[a, base + j] for j in range(BATCH)]
        live_count = live_counts[a]
        lives = [flag(base + j < live_count) for j in range(BATCH)]
        re, im = probe[0], probe[1]
        exits = []
        for j in range(BATCH):
            obj_re = reach[a, 0, pl.ds(offsets[j], pw), :]
            obj_im = reach[a, 1, pl.ds(offsets[j], pw), :]
            exits.append(
                jnp.concatenate(
                    [re * obj_re - im * obj_im, re * obj_im + im * obj_re], axis=0
                ).astype(jnp.bfloat16)
            )
        done = dot(minus[...], jnp.concatenate(exits, axis=1)).astype(jnp.bfloat16)
        done = jnp.concatenate(
            [
                jnp.concatenate(
                    [
                        done[:pw, j * rows : (j + 1) * rows],
                        done[pw:, j * rows : (j + 1) * rows],
                    ],
                    axis=1,
                )
                for j in range(BATCH)
            ],
            axis=0,
        )
        spectrum = dot(done, plus[...])
        s_re, s_im = spectrum[:, :rows], spectrum[:, rows:]
        counts = counts_v[a, pl.ds(base, BATCH)].astype(jnp.float32).reshape(BATCH * pw, rows)
        power = 256.0 * (s_re * s_re + s_im * s_im) + 64.0
        factor = counts * lax.rsqrt(jnp.maximum(counts * power, 1e-20))
        replaced = jnp.concatenate([s_re * factor, s_im * factor], axis=1).astype(jnp.bfloat16)
        inverse = dot(replaced, minus[...]).astype(jnp.bfloat16)
        inverse = jnp.concatenate(
            [
                jnp.concatenate(
                    [
                        inverse[j * pw : (j + 1) * pw, :rows],
                        inverse[j * pw : (j + 1) * pw, rows:],
                    ],
                    axis=0,
                )
                for j in range(BATCH)
            ],
            axis=1,
        )
        wave = dot(plus[...], inverse)
        for j in range(BATCH):
            diff = wave[:, j * rows : (j + 1) * rows] - exits[j].astype(jnp.float32)
            d_re, d_im = diff[:pw] * lives[j], diff[pw:] * lives[j]
            patch_tmp[j, 0, cols : cols + pw, :] = re * d_re + im * d_im
            patch_tmp[j, 1, cols : cols + pw, :] = re * d_im - im * d_re
        for plane in range(2):
            total = acc[a, plane]
            for j in range(BATCH):
                total = total + patch_tmp[j, plane, pl.ds(cols - offsets[j], 3 * cols), :]
            acc[a, plane] = total
        total = acc[a, 2]
        for j in range(BATCH):
            total = total + power_tmp[pl.ds(cols - offsets[j], 3 * cols), :] * lives[j]
        acc[a, 2] = total

    def update_copy(a, k):
        return remote(
            upd_out.at[a, k - 1],
            upd_in.at[a, k - 1],
            upd_send.at[a, k - 1],
            upd_recv.at[a, k - 1],
            v,
            tile_at(k),
        )

    def run_patches(a, first, last):
        nonlocal pumped
        each = min(PUMP[2], (pieces - pumped) // (last - first))
        base = pumped

        def body(b, _):
            pump(base + (b - first) * each, each)
            patches(a, b)
            return 0

        lax.fori_loop(first, last, body, 0)
        pumped += each * (last - first)

    def send_update(a):
        for k in (1, 2):
            upd_out[a, k - 1] = acc[a, :, k * cols : (k + 1) * cols, :].astype(jnp.bfloat16)
            update_copy(a, k).start()

    from_one, from_two = flag(t >= 1), flag(t >= 2)

    def finish_object(a):
        for step in range(1, group):
            group_copy(step, a).wait()
        for k in (1, 2):
            update_copy(a, k).wait()
        upd = (
            acc[a, :, :cols, :]
            + upd_in[a, 0].astype(jnp.float32) * from_one
            + upd_in[a, 1].astype(jnp.float32) * from_two
        )
        scale = 1.0 / (1.0 + upd[2])
        for k in range(2):
            projection = level_sum(t, place, a, k)
            for step in range(1, group):
                projection = projection + shared_in[step - 1, a, k].astype(jnp.float32)
            obj = reach[a, k, :cols, :]
            dual = dual_v[a, k]
            new = obj + upd[k] * scale - rho_weight * (obj - projection - dual)
            object_out[a, k] = new
            dual_new = dual + projection - new
            dual_out[a, k] = dual_new
            resid_full[a][t, k] = dual_new.astype(jnp.bfloat16)

    def source_at(lane, tile):
        k, j = lane // 2, lane % 2
        base = lax.rem(tile // group - k + levels, levels) * group
        spot = lax.rem(tile, group)
        return base + (lax.rem(spot + 2, group) if j else spot)

    lanes = 2 * levels

    def resid_copy(a, lane, source, to):
        return remote(
            resid_full[a].at[source],
            resid_full[a].at[source],
            res_send.at[a, lane],
            res_recv.at[a, lane],
            v,
            to,
        )

    def relay_copy(a, lane, source):
        return remote(
            resid_full[a].at[source],
            resid_full[a].at[source],
            rel_send.at[a, lane],
            rel_recv.at[a, lane],
            v,
            sibling,
        )

    def send_resid(a):
        resid_copy(a, 1, t, beside).start()
        for k in range(1, levels):
            resid_copy(a, 2 * k, t, level_at(k) * group + place).start()
        relay_copy(a, 0, t).start()

    def relay_resid(a):
        resid_copy(a, 1, beside, beside).wait_recv()
        for k in range(1, levels):
            resid_copy(a, 2 * k + 1, beside, level_at(k) * group + place).start()
        relay_copy(a, 1, beside).start()
        for lane in range(2, lanes):
            source = source_at(lane, t)
            resid_copy(a, lane, source, t).wait_recv()
            relay_copy(a, lane, source).start()

    def rt_part(k, a):
        return rt.at[k, :, pl.ds(a * 2 * cols, 2 * cols)]

    def rt_copy(a, lane, to):
        return remote(
            rt_part(0, a),
            rt_part(lane, a),
            rt_send.at[a, lane - 1],
            rt_recv.at[a, lane - 1],
            to,
            t,
        )

    def send_windows(a):
        for lane in range(lanes):
            relay_copy(a, lane, source_at(lane, sibling)).wait_recv()
            relay_copy(a, lane, source_at(lane, t)).wait_send()
        for lane in range(1, lanes):
            resid_copy(a, lane, t, t).wait_send()
        for k in range(2):
            window = jnp.concatenate(
                [resid_full[a][foot[a], k], resid_full[a][foot[a] + 1, k]], axis=0
            )
            rt[0, k * rows : (k + 1) * rows, a * 2 * cols : (a + 1) * 2 * cols] = (
                window.astype(jnp.float32).T.astype(jnp.bfloat16)
            )
        for k in range(1, nv // 2):
            rt_copy(a, k, view_at(2 * k)).start()

    batches = slots // BATCH
    for a in range(views):
        loads[2 + a].wait()
        run_patches(a, 0, batches)
        send_update(a)
        share_sums(a)
    pump_some(PUMP[3])
    for a in range(views):
        finish_object(a)
        send_resid(a)
    pump_some(PUMP[4])
    for a in range(views):
        relay_resid(a)
    pump_some(PUMP[5])
    for a in range(views):
        send_windows(a)
    pump_some(pieces)

    base = pl.multiple_of((v // 2) * wide_span, wide_span)

    def product(lane, side):
        at = pl.multiple_of(side * span, span)
        if lane:
            block = weights_in[lane - 1, :, :, pl.ds(at, span)]
        else:
            block = weights_v[:, :, pl.ds(base + at, span)]
        return dot(rt[lane], block.reshape(views * 2 * cols, span))

    grad[0] = product(0, 1 - view_x)
    grad[1] = product(0, view_x)
    for lane in range(1, nv // 2):
        for a in range(views):
            rt_copy(a, lane, v).wait()
        remote(
            weights_hbm.at[:, :, pl.ds(0, wide_span)],
            weights_in.at[lane - 1],
            w_send.at[lane - 1],
            w_recv.at[lane - 1],
            v,
            t,
        ).wait()
        grad[0] += product(lane, 1 - view_x)
        if lane < nv // 2 - 1:
            grad[1] += product(lane, view_x)

    def pair_copy(part):
        return remote(
            pair_out.at[part], pair_in.at[part], pair_send.at[part], pair_recv.at[part], over, t
        )

    half_span = span // 2
    for part in range(2):
        pair_out[part] = grad[0, :, part * half_span : (part + 1) * half_span].astype(jnp.bfloat16)
        pair_copy(part).start()
    grad[1] += product(nv // 2 - 1, view_x)
    def take_pair(part):
        pair_copy(part).wait()
        for c in range(part * share_cols // 2, (part + 1) * share_cols // 2):
            in_part = c * depth - part * half_span
            for k in range(2):
                both = grad[1, k * rows : (k + 1) * rows, c * depth : (c + 1) * depth] + pair_in[
                    part, k * rows : (k + 1) * rows, in_part : in_part + depth
                ].astype(jnp.float32)
                half[k, c] = volume_v[k, v * share_cols + c] - step_size * both.T

    row = lax.broadcasted_iota(jnp.int32, (depth, rows), 0)
    lane = lax.broadcasted_iota(jnp.int32, (depth, rows), 1)

    def inner(x):
        below = jnp.where(row == 0, 0.0, pltpu.roll(x, 1, 0))
        above = jnp.where(row == depth - 1, 0.0, pltpu.roll(x, depth - 1, 0))
        left = jnp.where(lane == 0, 0.0, pltpu.roll(x, 1, 1))
        right = jnp.where(lane == rows - 1, 0.0, pltpu.roll(x, rows - 1, 1))
        return phi(x - below) + phi(x - above) + phi(x - left) + phi(x - right)

    def finish(k, c, slot, before, after):
        x = half[k, c]
        prior = inner(x) + phi(x - before) + phi(x - after)
        share[k, slot] = (x - (step_size * prior_weight) * prior).astype(jnp.bfloat16)

    up, down, across = view_at(2), view_at(-2), view_at(4)
    other_up, other_down = lax.rem(over + 2, nv), lax.rem(over - 2 + nv, nv)
    other_across = lax.rem(over + 4, nv)
    early = share_cols // 2 - 2
    spans = (
        pl.ds(0, early),
        pl.ds(early, share_cols - 2 - early),
        pl.ds(share_cols - 2, 2),
    )
    sent = []

    def go(copy):
        copy.start()
        sent.append(copy)

    def hand_on(source, k, part, lane, to):
        return remote(
            gathered.at[source, k, spans[part]],
            gathered.at[source, k, spans[part]],
            ag_send.at[lane, k, part],
            ag_recv.at[lane, k, part],
            to,
            t,
        )

    def own(k, part, lane, to):
        return remote(
            share.at[k, spans[part]],
            gathered.at[v, k, spans[part]],
            ag_send.at[lane, k, part],
            ag_recv.at[lane, k, part],
            to,
            t,
        )

    def send_own(k, part):
        go(own(k, part, 0, up))
        go(own(k, part, 1, down))
        go(own(k, part, 2, over))

    def finish_inner(k, first, last):
        lax.fori_loop(
            first,
            last,
            lambda c, _: (finish(k, c, c - 1, half[k, c - 1], half[k, c + 1]), 0)[1],
            0,
        )

    take_pair(0)
    for k in range(2):
        finish_inner(k, 1, early + 1)
        send_own(k, 0)
    take_pair(1)
    for k in range(2):
        halo_out[0, k] = half[k, 0].astype(jnp.bfloat16)
        halo_out[1, k] = half[k, share_cols - 1].astype(jnp.bfloat16)
    halo_copies = [
        remote(halo_out.at[0], halo_in.at[1], halo_send.at[0], halo_recv.at[1], back_v, back_t),
        remote(halo_out.at[1], halo_in.at[0], halo_send.at[1], halo_recv.at[0], fore_v, fore_t),
    ]
    for copy in halo_copies:
        copy.start()
    for k in range(2):
        finish_inner(k, early + 1, share_cols - 1)
        send_own(k, 1)
    for copy in halo_copies:
        copy.wait()
    has_back = flag((v > 0) | (t > 0))
    has_fore = flag((v < nv - 1) | (t < nt - 1))
    for k in range(2):
        finish(k, 0, share_cols - 2, halo_in[0, k].astype(jnp.float32) * has_back, half[k, 1])
        finish(
            k,
            share_cols - 1,
            share_cols - 1,
            half[k, share_cols - 2],
            halo_in[1, k].astype(jnp.float32) * has_fore,
        )
        send_own(k, 2)

    own_copy = pltpu.make_async_copy(share, gathered.at[v], local_sem.at[5 + views])
    own_copy.start()
    for part in range(3):
        for k in range(2):
            if k == 0:
                hand_on(down, 0, part, 0, up).wait_recv()
                go(hand_on(down, 0, part, 3, up))
            else:
                hand_on(up, 1, part, 1, down).wait_recv()
                go(hand_on(up, 1, part, 3, down))
            hand_on(over, k, part, 2, over).wait_recv()
            go(hand_on(over, k, part, 4, up))
            go(hand_on(over, k, part, 5, down))
    for part in range(3):
        for k in range(2):
            hand_on(across, k, part, 3, up).wait_recv()
            go(hand_on(across, k, part, 6, over))
    for part in range(3):
        hand_on(down, 1, part, 0, up).wait_recv()
        hand_on(up, 0, part, 1, up).wait_recv()
        for k in range(2):
            hand_on(other_down, k, part, 4, up).wait_recv()
            hand_on(other_up, k, part, 5, down).wait_recv()
            hand_on(other_across, k, part, 6, over).wait_recv()
    for copy in sent:
        copy.wait_send()
    own_copy.wait()


def widen_kernel(object_ref, dual_ref, gathered, object_out, dual_out, volume_out, low, wide, in_sem, out_sem):
    parts, _, share_cols = gathered.shape[:3]

    def load(i):
        return pltpu.make_async_copy(gathered.at[i], low.at[i], in_sem.at[i])

    def store(i):
        return pltpu.make_async_copy(
            wide.at[i], volume_out.at[:, pl.ds(i * share_cols, share_cols)], out_sem.at[i]
        )

    for i in range(parts):
        load(i).start()
    object_out[...] = object_ref[...]
    dual_out[...] = dual_ref[...]

    def step(i, _):
        load(i).wait()
        wide[i, :, 1 : share_cols - 1] = low[i, :, : share_cols - 2].astype(jnp.float32)
        wide[i, :, 0] = low[i, :, share_cols - 2].astype(jnp.float32)
        wide[i, :, share_cols - 1] = low[i, :, share_cols - 1].astype(jnp.float32)
        store(i).start()
        return 0

    lax.fori_loop(0, parts, step, 0)
    for i in range(parts):
        store(i).wait()


def per_device(
    nv,
    nt,
    object_band,
    dual_band,
    probe_field,
    positions,
    live_counts,
    photon_counts,
    footprints,
    weights,
    volume,
):
    views, _, cols, rows = object_band.shape
    pw = probe_field.shape[1]
    slots = positions.shape[1]
    depth = volume.shape[2]
    share_cols = cols // nv
    span = share_cols * depth
    minus, plus = dft_tables(pw)
    hbm = pl.BlockSpec(memory_space=pltpu.HBM)
    smem = pl.BlockSpec(memory_space=pltpu.SMEM)
    vmem = pl.BlockSpec(memory_space=pltpu.VMEM)
    bf16, f32 = jnp.bfloat16, jnp.float32
    dma = pltpu.SemaphoreType.DMA
    levels = nt // 4
    band = jax.ShapeDtypeStruct(object_band.shape, f32)
    object_new, dual_new, gathered = pl.pallas_call(
        functools.partial(front_kernel, nv, nt),
        out_shape=(
            band,
            band,
            jax.ShapeDtypeStruct((nv, 2, share_cols, depth, rows), bf16),
        ),
        in_specs=[smem] * 3 + [hbm] * 8,
        out_specs=(vmem, vmem, hbm),
        scratch_shapes=[
            pltpu.VMEM(probe_field.shape, f32),
            pltpu.VMEM(minus.shape, bf16),
            pltpu.VMEM(plus.shape, bf16),
            pltpu.VMEM((views, 2, cols, rows), f32),
            pltpu.VMEM((views, 2, 3 * cols, rows), f32),
            pltpu.VMEM((views, slots, pw, rows), jnp.int32),
            pltpu.VMEM(weights.shape, bf16),
            pltpu.VMEM(volume.shape, f32),
            pltpu.VMEM((nv // 2 - 1, views, 2 * cols, 2 * span), bf16),
            pltpu.VMEM((views * 2 * cols, 2 * rows), f32),
            pltpu.VMEM((levels - 1, views, 4, 2, cols, rows), bf16),
            pltpu.VMEM((levels - 1, views, 4, 2, cols, rows), bf16),
            pltpu.VMEM((3, views, 2, cols, rows), bf16),
            pltpu.VMEM((3, views, 2, cols, rows), bf16),
            pltpu.VMEM((BATCH, 2, 4 * cols, rows), f32),
            pltpu.VMEM((4 * cols, rows), f32),
            pltpu.VMEM((views, 3, 3 * cols, rows), f32),
            pltpu.VMEM((views, 2, 3, cols, rows), bf16),
            pltpu.VMEM((views, 2, 3, cols, rows), bf16),
            pltpu.VMEM((nt, 2, cols, rows), bf16),
            pltpu.VMEM((nt, 2, cols, rows), bf16),
            pltpu.VMEM((nv // 2, 2 * rows, views * 2 * cols), bf16),
            pltpu.VMEM((2, 2 * rows, span), f32),
            pltpu.VMEM((2, 2 * rows, span // 2), bf16),
            pltpu.VMEM((2, 2 * rows, span // 2), bf16),
            pltpu.VMEM((2, share_cols, depth, rows), f32),
            pltpu.VMEM((2, 2, depth, rows), bf16),
            pltpu.VMEM((2, 2, depth, rows), bf16),
            pltpu.VMEM((2, share_cols, depth, rows), bf16),
            dma((6 + views,)),
            dma((2, nv)),
            dma((nv // 2 - 1,)),
            dma((nv // 2 - 1,)),
            dma((2,)),
            dma((2,)),
            dma((levels - 1, views)),
            dma((levels - 1, views)),
            dma((3, views)),
            dma((3, views)),
            dma((views, 2)),
            dma((views, 2)),
            dma((views, 2 * levels)),
            dma((views, 2 * levels)),
            dma((views, 2 * levels)),
            dma((views, 2 * levels)),
            dma((views, nv // 2 - 1)),
            dma((views, nv // 2 - 1)),
            dma((2,)),
            dma((2,)),
            dma((2,)),
            dma((2,)),
            dma((7, 2, 3)),
            dma((7, 2, 3)),
        ],
        compiler_params=pltpu.CompilerParams(
            collective_id=0, has_side_effects=True, vmem_limit_bytes=FRONT_VMEM * MIB
        ),
        name="front",
    )(
        positions,
        live_counts.reshape(views),
        footprints.reshape(views),
        object_band,
        dual_band,
        probe_field,
        minus,
        plus,
        photon_counts,
        weights,
        volume,
    )
    return pl.pallas_call(
        widen_kernel,
        out_shape=(band, band, jax.ShapeDtypeStruct(volume.shape, f32)),
        in_specs=[vmem, vmem, hbm],
        out_specs=(vmem, vmem, hbm),
        scratch_shapes=[
            pltpu.VMEM(gathered.shape, bf16),
            pltpu.VMEM(gathered.shape, f32),
            dma((nv,)),
            dma((nv,)),
        ],
        compiler_params=pltpu.CompilerParams(vmem_limit_bytes=WIDEN_VMEM * MIB),
        name="widen",
    )(object_new, dual_new, gathered)


def solution(mesh):
    return jax.shard_map(
        functools.partial(per_device, mesh.shape["view"], mesh.shape["tile"]),
        mesh=mesh,
        in_specs=(
            P("view", None, "tile", None),
            P("view", None, "tile", None),
            P(),
            P("view", "tile"),
            P("view", "tile"),
            P("view", "tile", None, None),
            P("view", "tile"),
            P("view", None, "tile"),
            P(None, "tile", None, None),
        ),
        out_specs=(
            P("view", None, "tile", None),
            P("view", None, "tile", None),
            P(None, "tile", None, None),
        ),
        check_vma=False,
    )
```

```python
import functools

import jax
import jax.numpy as jnp
import numpy as np
from jax import lax
from jax.experimental import pallas as pl
from jax.experimental.pallas import tpu as pltpu
from jax.sharding import PartitionSpec as P

rho_weight = 0.5
step_size = 0.5
prior_weight = 0.5
MESH = pl.DeviceIdType.MESH
BATCH = 4
PIECE_ROWS = 128
FRONT_VMEM = 60
WIDEN_VMEM = 60
PUMP = (6, 0, 0, 0, 0, 0)
MIB = 2**20


def dft_tables(order):
    counter = np.arange(order)
    angles = ((counter[:, None] * counter[None, :]) % order).astype(np.float32)
    angles = angles * np.float32(2.0 * np.pi / order)
    scaling = np.float32(1.0 / np.sqrt(np.float32(order)))
    re, im = np.cos(angles) * scaling, -np.sin(angles) * scaling
    minus = np.block([[re, -im], [im, re]])
    plus = np.block([[re, im], [-im, re]])
    return jnp.asarray(minus, jnp.bfloat16), jnp.asarray(plus, jnp.bfloat16)


def phi(d):
    return d * lax.rsqrt(1.0 + d * d)


def flag(condition):
    return jnp.where(condition, jnp.float32(1.0), jnp.float32(0.0))


def dot(a, b):
    return jnp.dot(a, b, preferred_element_type=jnp.float32)


def front_kernel(
    nv,
    nt,
    positions,
    live_counts,
    footprints,
    object_hbm,
    dual_hbm,
    probe_hbm,
    minus_hbm,
    plus_hbm,
    counts_hbm,
    weights_hbm,
    volume_hbm,
    object_out,
    dual_out,
    gathered,
    probe,
    minus,
    plus,
    dual_v,
    reach,
    counts_v,
    weights_v,
    volume_v,
    weights_in,
    shadow,
    shadow_out,
    shadow_in,
    shared_out,
    shared_in,
    patch_tmp,
    power_tmp,
    acc,
    upd_out,
    upd_in,
    resid_first,
    resid_second,
    rt,
    grad,
    pair_out,
    pair_in,
    half,
    halo_out,
    halo_in,
    share,
    local_sem,
    chunk_sem,
    w_send,
    w_recv,
    obj_send,
    obj_recv,
    sh_send,
    sh_recv,
    gr_send,
    gr_recv,
    upd_send,
    upd_recv,
    res_send,
    res_recv,
    rel_send,
    rel_recv,
    rt_send,
    rt_recv,
    pair_send,
    pair_recv,
    halo_send,
    halo_recv,
    ag_send,
    ag_recv,
):
    v = lax.axis_index("view")
    t = lax.axis_index("tile")
    views, slots = positions.shape
    resid_full = (resid_first, resid_second)
    cols = reach.shape[2] // 3
    depth = volume_hbm.shape[2]
    share_cols = cols // nv
    span = share_cols * depth
    rows = probe.shape[2]
    pw = probe.shape[1]

    def remote(src, dst, send, recv, view, tile):
        return pltpu.make_async_remote_copy(
            src_ref=src,
            dst_ref=dst,
            send_sem=send,
            recv_sem=recv,
            device_id={"view": view, "tile": tile},
            device_id_type=MESH,
        )

    def view_at(k):
        return lax.rem(v + k + nv, nv)

    def tile_at(k):
        return lax.rem(t + k + nt, nt)

    group = 4
    levels = nt // group
    z, place = t // group, lax.rem(t, group)
    core = lax.rem(t, 2)
    sibling = t + 1 - 2 * core
    beside = t + 2 - 4 * (place // 2)
    view_x = lax.rem(v, 2)
    over = v + 1 - 2 * view_x

    def level_at(k):
        return lax.rem(z + k + levels, levels)

    back_v, back_t = view_at(-1), jnp.where(v == 0, tile_at(-1), t)
    fore_v, fore_t = view_at(1), jnp.where(v == nv - 1, tile_at(1), t)

    loads = [
        pltpu.make_async_copy(object_hbm, reach.at[:, :, pl.ds(0, cols), :], local_sem.at[0]),
        pltpu.make_async_copy(dual_hbm, dual_v, local_sem.at[1]),
    ]
    for a in range(views):
        loads.append(
            pltpu.make_async_copy(counts_hbm.at[a], counts_v.at[a], local_sem.at[2 + a])
        )
    for i, (source, target) in enumerate(
        ((probe_hbm, probe), (minus_hbm, minus), (plus_hbm, plus))
    ):
        loads.append(pltpu.make_async_copy(source, target, local_sem.at[2 + views + i]))

    def chunk_copies(c):
        first = pl.multiple_of(c * span, span)
        return (
            pltpu.make_async_copy(
                weights_hbm.at[:, :, pl.ds(first, span)],
                weights_v.at[:, :, pl.ds(first, span)],
                chunk_sem.at[0, c],
            ),
            pltpu.make_async_copy(
                volume_hbm.at[:, pl.ds(c * share_cols, share_cols)],
                volume_v.at[:, pl.ds(c * share_cols, share_cols)],
                chunk_sem.at[1, c],
            ),
        )

    loads[0].start()
    for c in range(nv):
        for copy in chunk_copies(c):
            copy.start()
    for copy in loads[1:]:
        copy.start()

    barrier = pltpu.get_barrier_semaphore()

    def greet(view, tile):
        pl.semaphore_signal(
            barrier, inc=1, device_id={"view": view, "tile": tile}, device_id_type=MESH
        )

    for k in range(1, nv):
        greet(view_at(k), t)
    for k in range(1, nt):
        greet(v, tile_at(k))
    greet(back_v, back_t)
    greet(fore_v, fore_t)
    pl.semaphore_wait(barrier, nv + nt)

    object_copies = [
        remote(
            object_hbm,
            reach.at[:, :, pl.ds(k * cols, cols), :],
            obj_send.at[k - 1],
            obj_recv.at[k - 1],
            v,
            tile_at(-k),
        )
        for k in (1, 2)
    ]
    for copy in object_copies:
        copy.start()

    peers = nv // 2 - 1
    piece_rows = PIECE_ROWS
    wide_span = 2 * span
    per_view = 2 * cols // piece_rows
    pieces = peers * views * per_view

    def pump(first, count):
        for extra in range(count):
            index = first + extra
            k = index % peers
            row_block = index // peers
            a = row_block // per_view
            rows_at = pl.multiple_of((row_block % per_view) * piece_rows, piece_rows)
            to = lax.rem(v + 2 * (k + 1), nv)
            first_voxel = pl.multiple_of((to // 2) * wide_span, wide_span)
            remote(
                weights_hbm.at[a, pl.ds(rows_at, piece_rows), pl.ds(first_voxel, wide_span)],
                weights_in.at[k, a, pl.ds(rows_at, piece_rows), :],
                w_send.at[k],
                w_recv.at[k],
                to,
                t,
            ).start()

    pumped = 0

    def pump_some(count):
        nonlocal pumped
        count = min(count, pieces - pumped)
        pump(pumped, count)
        pumped += count

    pump_some(PUMP[0])

    shadow[...] = jnp.zeros_like(shadow)

    def project(c, _):
        for copy in chunk_copies(c):
            copy.wait()
        first = pl.multiple_of(c * span, span)
        left = weights_v[:, :, pl.ds(first, span)].reshape(views * 2 * cols, span)
        block = volume_v[:, pl.ds(c * share_cols, share_cols)].astype(jnp.bfloat16)
        right = jnp.concatenate(
            [block[0].reshape(span, rows), block[1].reshape(span, rows)], axis=1
        )
        shadow[...] += dot(left, right)
        return 0

    lax.fori_loop(0, nv, project, 0)

    foot = [footprints[a] for a in range(views)]

    def shadow_part(a, k, part):
        first = a * 2 * cols + part * cols
        return shadow[first : first + cols, k * rows : (k + 1) * rows]

    def placed(to, a, k):
        return shadow_part(a, k, 0) * flag(foot[a] == to) + shadow_part(a, k, 1) * flag(
            foot[a] + 1 == to
        )

    def level_copy(k, a):
        return remote(
            shadow_out.at[k - 1, a],
            shadow_in.at[k - 1, a],
            sh_send.at[k - 1, a],
            sh_recv.at[k - 1, a],
            v,
            level_at(k) * group + place,
        )

    def group_copy(k, a):
        return remote(
            shared_out.at[k - 1, a],
            shared_in.at[k - 1, a],
            gr_send.at[k - 1, a],
            gr_recv.at[k - 1, a],
            v,
            z * group + lax.rem(place + k, group),
        )

    for a in range(views):
        for step in range(1, levels):
            for k in range(group):
                to = level_at(step) * group + k
                for plane in range(2):
                    shadow_out[step - 1, a, k, plane] = placed(to, a, plane).astype(jnp.bfloat16)
            level_copy(step, a).start()

    def level_sum(to, k, a, plane):
        total = placed(to, a, plane)
        for step in range(1, levels):
            total = total + shadow_in[step - 1, a, k, plane].astype(jnp.float32)
        return total

    def share_sums(a):
        for step in range(1, levels):
            level_copy(step, a).wait()
        for step in range(1, group):
            k = lax.rem(place + step, group)
            for plane in range(2):
                shared_out[step - 1, a, plane] = level_sum(z * group + k, k, a, plane).astype(
                    jnp.bfloat16
                )
            group_copy(step, a).start()

    pump_some(PUMP[1])

    for copy in loads[2 + views :]:
        copy.wait()
    probe_re, probe_im = probe[0], probe[1]
    acc[...] = jnp.zeros_like(acc)
    patch_tmp[...] = jnp.zeros_like(patch_tmp)
    power_tmp[...] = jnp.zeros_like(power_tmp)
    power_tmp[cols : cols + pw, :] = probe_re * probe_re + probe_im * probe_im
    for copy in loads[:2]:
        copy.wait()
    for copy in object_copies:
        copy.wait()
    for k in (1, 2):
        inside = flag(t + k < nt)
        for a in range(views):
            for plane in range(2):
                reach[a, plane, k * cols : (k + 1) * cols, :] = (
                    reach[a, plane, k * cols : (k + 1) * cols, :] * inside
                )

    def patches(a, b):
        base = b * BATCH
        offsets = [positions[a, base + j] for j in range(BATCH)]
        live_count = live_counts[a]
        lives = [flag(base + j < live_count) for j in range(BATCH)]
        re, im = probe[0], probe[1]
        exits = []
        for j in range(BATCH):
            obj_re = reach[a, 0, pl.ds(offsets[j], pw), :]
            obj_im = reach[a, 1, pl.ds(offsets[j], pw), :]
            exits.append(
                jnp.concatenate(
                    [re * obj_re - im * obj_im, re * obj_im + im * obj_re], axis=0
                ).astype(jnp.bfloat16)
            )
        done = dot(minus[...], jnp.concatenate(exits, axis=1)).astype(jnp.bfloat16)
        done = jnp.concatenate(
            [
                jnp.concatenate(
                    [
                        done[:pw, j * rows : (j + 1) * rows],
                        done[pw:, j * rows : (j + 1) * rows],
                    ],
                    axis=1,
                )
                for j in range(BATCH)
            ],
            axis=0,
        )
        spectrum = dot(done, plus[...])
        s_re, s_im = spectrum[:, :rows], spectrum[:, rows:]
        counts = counts_v[a, pl.ds(base, BATCH)].astype(jnp.float32).reshape(BATCH * pw, rows)
        power = 256.0 * (s_re * s_re + s_im * s_im) + 64.0
        factor = counts * lax.rsqrt(jnp.maximum(counts * power, 1e-20))
        replaced = jnp.concatenate([s_re * factor, s_im * factor], axis=1).astype(jnp.bfloat16)
        inverse = dot(replaced, minus[...]).astype(jnp.bfloat16)
        inverse = jnp.concatenate(
            [
                jnp.concatenate(
                    [
                        inverse[j * pw : (j + 1) * pw, :rows],
                        inverse[j * pw : (j + 1) * pw, rows:],
                    ],
                    axis=0,
                )
                for j in range(BATCH)
            ],
            axis=1,
        )
        wave = dot(plus[...], inverse)
        for j in range(BATCH):
            diff = wave[:, j * rows : (j + 1) * rows] - exits[j].astype(jnp.float32)
            d_re, d_im = diff[:pw] * lives[j], diff[pw:] * lives[j]
            patch_tmp[j, 0, cols : cols + pw, :] = re * d_re + im * d_im
            patch_tmp[j, 1, cols : cols + pw, :] = re * d_im - im * d_re
        for plane in range(2):
            total = acc[a, plane]
            for j in range(BATCH):
                total = total + patch_tmp[j, plane, pl.ds(cols - offsets[j], 3 * cols), :]
            acc[a, plane] = total
        total = acc[a, 2]
        for j in range(BATCH):
            total = total + power_tmp[pl.ds(cols - offsets[j], 3 * cols), :] * lives[j]
        acc[a, 2] = total

    def update_copy(a, k):
        return remote(
            upd_out.at[a, k - 1],
            upd_in.at[a, k - 1],
            upd_send.at[a, k - 1],
            upd_recv.at[a, k - 1],
            v,
            tile_at(k),
        )

    def run_patches(a, first, last):
        nonlocal pumped
        each = min(PUMP[2], (pieces - pumped) // (last - first))
        base = pumped

        def body(b, _):
            pump(base + (b - first) * each, each)
            patches(a, b)
            return 0

        lax.fori_loop(first, last, body, 0)
        pumped += each * (last - first)

    def send_update(a):
        for k in (1, 2):
            upd_out[a, k - 1] = acc[a, :, k * cols : (k + 1) * cols, :].astype(jnp.bfloat16)
            update_copy(a, k).start()

    from_one, from_two = flag(t >= 1), flag(t >= 2)

    def finish_object(a):
        for step in range(1, group):
            group_copy(step, a).wait()
        for k in (1, 2):
            update_copy(a, k).wait()
        upd = (
            acc[a, :, :cols, :]
            + upd_in[a, 0].astype(jnp.float32) * from_one
            + upd_in[a, 1].astype(jnp.float32) * from_two
        )
        scale = 1.0 / (1.0 + upd[2])
        for k in range(2):
            projection = level_sum(t, place, a, k)
            for step in range(1, group):
                projection = projection + shared_in[step - 1, a, k].astype(jnp.float32)
            obj = reach[a, k, :cols, :]
            dual = dual_v[a, k]
            new = obj + upd[k] * scale - rho_weight * (obj - projection - dual)
            object_out[a, k] = new
            dual_new = dual + projection - new
            dual_out[a, k] = dual_new
            resid_full[a][t, k] = dual_new.astype(jnp.bfloat16)

    def source_at(lane, tile):
        k, j = lane // 2, lane % 2
        base = lax.rem(tile // group - k + levels, levels) * group
        spot = lax.rem(tile, group)
        return base + (lax.rem(spot + 2, group) if j else spot)

    lanes = 2 * levels

    def resid_copy(a, lane, source, to):
        return remote(
            resid_full[a].at[source],
            resid_full[a].at[source],
            res_send.at[a, lane],
            res_recv.at[a, lane],
            v,
            to,
        )

    def relay_copy(a, lane, source):
        return remote(
            resid_full[a].at[source],
            resid_full[a].at[source],
            rel_send.at[a, lane],
            rel_recv.at[a, lane],
            v,
            sibling,
        )

    def send_resid(a):
        resid_copy(a, 1, t, beside).start()
        for k in range(1, levels):
            resid_copy(a, 2 * k, t, level_at(k) * group + place).start()
        relay_copy(a, 0, t).start()

    def forward_resid(a):
        resid_copy(a, 1, beside, beside).wait_recv()
        for k in range(1, levels):
            resid_copy(a, 2 * k + 1, beside, level_at(k) * group + place).start()
        relay_copy(a, 1, beside).start()
    def relay_resid(a, first):
        for lane in range(first, lanes, 2):
            source = source_at(lane, t)
            resid_copy(a, lane, source, t).wait_recv()
            relay_copy(a, lane, source).start()

    def rt_part(k, a):
        return rt.at[k, :, pl.ds(a * 2 * cols, 2 * cols)]

    def rt_copy(a, lane, to):
        return remote(
            rt_part(0, a),
            rt_part(lane, a),
            rt_send.at[a, lane - 1],
            rt_recv.at[a, lane - 1],
            to,
            t,
        )

    def send_windows(a):
        for lane in range(lanes):
            relay_copy(a, lane, source_at(lane, sibling)).wait_recv()
            relay_copy(a, lane, source_at(lane, t)).wait_send()
        for lane in range(1, lanes):
            resid_copy(a, lane, t, t).wait_send()
        for k in range(2):
            window = jnp.concatenate(
                [resid_full[a][foot[a], k], resid_full[a][foot[a] + 1, k]], axis=0
            )
            rt[0, k * rows : (k + 1) * rows, a * 2 * cols : (a + 1) * 2 * cols] = (
                window.astype(jnp.float32).T.astype(jnp.bfloat16)
            )
        for k in range(1, nv // 2):
            rt_copy(a, k, view_at(2 * k)).start()

    batches = slots // BATCH
    loads[2].wait()
    run_patches(0, 0, batches)
    send_update(0)
    loads[3].wait()
    run_patches(1, 0, batches // 2)
    share_sums(0)
    run_patches(1, batches // 2, batches)
    send_update(1)
    share_sums(1)
    pump_some(PUMP[3])
    for a in range(views):
        finish_object(a)
        send_resid(a)
    pump_some(PUMP[4])
    for a in range(views):
        forward_resid(a)
    for first in (2, 3):
        for a in range(views):
            relay_resid(a, first)
    pump_some(PUMP[5])
    for a in range(views):
        send_windows(a)
    pump_some(pieces)

    base = pl.multiple_of((v // 2) * wide_span, wide_span)

    def product(lane, side):
        at = pl.multiple_of(side * span, span)
        if lane:
            block = weights_in[lane - 1, :, :, pl.ds(at, span)]
        else:
            block = weights_v[:, :, pl.ds(base + at, span)]
        return dot(rt[lane], block.reshape(views * 2 * cols, span))

    grad[0] = product(0, 1 - view_x)
    grad[1] = product(0, view_x)
    for lane in range(1, nv // 2):
        for a in range(views):
            rt_copy(a, lane, v).wait()
        remote(
            weights_hbm.at[:, :, pl.ds(0, wide_span)],
            weights_in.at[lane - 1],
            w_send.at[lane - 1],
            w_recv.at[lane - 1],
            v,
            t,
        ).wait()
        grad[0] += product(lane, 1 - view_x)
        if lane < nv // 2 - 1:
            grad[1] += product(lane, view_x)

    def pair_copy(part):
        return remote(
            pair_out.at[part], pair_in.at[part], pair_send.at[part], pair_recv.at[part], over, t
        )

    half_span = span // 2
    for part in range(2):
        pair_out[part] = grad[0, :, part * half_span : (part + 1) * half_span].astype(jnp.bfloat16)
        pair_copy(part).start()
    grad[1] += product(nv // 2 - 1, view_x)
    def take_pair(part):
        pair_copy(part).wait()
        for c in range(part * share_cols // 2, (part + 1) * share_cols // 2):
            in_part = c * depth - part * half_span
            for k in range(2):
                both = grad[1, k * rows : (k + 1) * rows, c * depth : (c + 1) * depth] + pair_in[
                    part, k * rows : (k + 1) * rows, in_part : in_part + depth
                ].astype(jnp.float32)
                half[k, c] = volume_v[k, v * share_cols + c] - step_size * both.T

    row = lax.broadcasted_iota(jnp.int32, (depth, rows), 0)
    lane = lax.broadcasted_iota(jnp.int32, (depth, rows), 1)

    def inner(x):
        below = jnp.where(row == 0, 0.0, pltpu.roll(x, 1, 0))
        above = jnp.where(row == depth - 1, 0.0, pltpu.roll(x, depth - 1, 0))
        left = jnp.where(lane == 0, 0.0, pltpu.roll(x, 1, 1))
        right = jnp.where(lane == rows - 1, 0.0, pltpu.roll(x, rows - 1, 1))
        return phi(x - below) + phi(x - above) + phi(x - left) + phi(x - right)

    def finish(k, c, slot, before, after):
        x = half[k, c]
        prior = inner(x) + phi(x - before) + phi(x - after)
        share[k, slot] = (x - (step_size * prior_weight) * prior).astype(jnp.bfloat16)

    up, down, across = view_at(2), view_at(-2), view_at(4)
    other_up, other_down = lax.rem(over + 2, nv), lax.rem(over - 2 + nv, nv)
    other_across = lax.rem(over + 4, nv)
    early = share_cols // 2 - 2
    spans = (
        pl.ds(0, early),
        pl.ds(early, share_cols - 2 - early),
        pl.ds(share_cols - 2, 2),
    )
    sent = []

    def go(copy):
        copy.start()
        sent.append(copy)

    def hand_on(source, k, part, lane, to):
        return remote(
            gathered.at[source, k, spans[part]],
            gathered.at[source, k, spans[part]],
            ag_send.at[lane, k, part],
            ag_recv.at[lane, k, part],
            to,
            t,
        )

    def own(k, part, lane, to):
        return remote(
            share.at[k, spans[part]],
            gathered.at[v, k, spans[part]],
            ag_send.at[lane, k, part],
            ag_recv.at[lane, k, part],
            to,
            t,
        )

    def send_own(k, part):
        go(own(k, part, 0, up))
        go(own(k, part, 1, down))
        go(own(k, part, 2, over))

    def finish_inner(k, first, last):
        lax.fori_loop(
            first,
            last,
            lambda c, _: (finish(k, c, c - 1, half[k, c - 1], half[k, c + 1]), 0)[1],
            0,
        )

    take_pair(0)
    for k in range(2):
        finish_inner(k, 1, early + 1)
        send_own(k, 0)
    take_pair(1)
    for k in range(2):
        halo_out[0, k] = half[k, 0].astype(jnp.bfloat16)
        halo_out[1, k] = half[k, share_cols - 1].astype(jnp.bfloat16)
    halo_copies = [
        remote(halo_out.at[0], halo_in.at[1], halo_send.at[0], halo_recv.at[1], back_v, back_t),
        remote(halo_out.at[1], halo_in.at[0], halo_send.at[1], halo_recv.at[0], fore_v, fore_t),
    ]
    for copy in halo_copies:
        copy.start()
    for k in range(2):
        finish_inner(k, early + 1, share_cols - 1)
        send_own(k, 1)
    for copy in halo_copies:
        copy.wait()
    has_back = flag((v > 0) | (t > 0))
    has_fore = flag((v < nv - 1) | (t < nt - 1))
    for k in range(2):
        finish(k, 0, share_cols - 2, halo_in[0, k].astype(jnp.float32) * has_back, half[k, 1])
        finish(
            k,
            share_cols - 1,
            share_cols - 1,
            half[k, share_cols - 2],
            halo_in[1, k].astype(jnp.float32) * has_fore,
        )
        send_own(k, 2)

    own_copy = pltpu.make_async_copy(share, gathered.at[v], local_sem.at[5 + views])
    own_copy.start()
    for part in range(3):
        for k in range(2):
            if k == 0:
                hand_on(down, 0, part, 0, up).wait_recv()
                go(hand_on(down, 0, part, 3, up))
            else:
                hand_on(up, 1, part, 1, down).wait_recv()
                go(hand_on(up, 1, part, 3, down))
            hand_on(over, k, part, 2, over).wait_recv()
            go(hand_on(over, k, part, 4, up))
            go(hand_on(over, k, part, 5, down))
    for part in range(3):
        for k in range(2):
            hand_on(across, k, part, 3, up).wait_recv()
            go(hand_on(across, k, part, 6, over))
    for part in range(3):
        hand_on(down, 1, part, 0, up).wait_recv()
        hand_on(up, 0, part, 1, up).wait_recv()
        for k in range(2):
            hand_on(other_down, k, part, 4, up).wait_recv()
            hand_on(other_up, k, part, 5, down).wait_recv()
            hand_on(other_across, k, part, 6, over).wait_recv()
    for copy in sent:
        copy.wait_send()
    own_copy.wait()


def widen_kernel(object_ref, dual_ref, gathered, object_out, dual_out, volume_out, low, wide, in_sem, out_sem):
    parts, _, share_cols = gathered.shape[:3]

    def load(i, k):
        return pltpu.make_async_copy(gathered.at[i, k], low.at[i, k], in_sem.at[i, k])

    def store(i, k):
        return pltpu.make_async_copy(
            wide.at[i, k], volume_out.at[k, pl.ds(i * share_cols, share_cols)], out_sem.at[i, k]
        )

    for i in range(parts):
        for k in range(2):
            load(i, k).start()
    for i in range(parts):
        for k in range(2):
            load(i, k).wait()
            wide[i, k, 1 : share_cols - 1] = low[i, k, : share_cols - 2].astype(jnp.float32)
            wide[i, k, 0] = low[i, k, share_cols - 2].astype(jnp.float32)
            wide[i, k, share_cols - 1] = low[i, k, share_cols - 1].astype(jnp.float32)
            store(i, k).start()
    object_out[...] = object_ref[...]
    dual_out[...] = dual_ref[...]
    for i in range(parts):
        for k in range(2):
            store(i, k).wait()


def per_device(
    nv,
    nt,
    object_band,
    dual_band,
    probe_field,
    positions,
    live_counts,
    photon_counts,
    footprints,
    weights,
    volume,
):
    views, _, cols, rows = object_band.shape
    pw = probe_field.shape[1]
    slots = positions.shape[1]
    depth = volume.shape[2]
    share_cols = cols // nv
    span = share_cols * depth
    minus, plus = dft_tables(pw)
    hbm = pl.BlockSpec(memory_space=pltpu.HBM)
    smem = pl.BlockSpec(memory_space=pltpu.SMEM)
    vmem = pl.BlockSpec(memory_space=pltpu.VMEM)
    bf16, f32 = jnp.bfloat16, jnp.float32
    dma = pltpu.SemaphoreType.DMA
    levels = nt // 4
    band = jax.ShapeDtypeStruct(object_band.shape, f32)
    object_new, dual_new, gathered = pl.pallas_call(
        functools.partial(front_kernel, nv, nt),
        out_shape=(
            band,
            band,
            jax.ShapeDtypeStruct((nv, 2, share_cols, depth, rows), bf16),
        ),
        in_specs=[smem] * 3 + [hbm] * 8,
        out_specs=(vmem, vmem, hbm),
        scratch_shapes=[
            pltpu.VMEM(probe_field.shape, f32),
            pltpu.VMEM(minus.shape, bf16),
            pltpu.VMEM(plus.shape, bf16),
            pltpu.VMEM((views, 2, cols, rows), f32),
            pltpu.VMEM((views, 2, 3 * cols, rows), f32),
            pltpu.VMEM((views, slots, pw, rows), jnp.int32),
            pltpu.VMEM(weights.shape, bf16),
            pltpu.VMEM(volume.shape, f32),
            pltpu.VMEM((nv // 2 - 1, views, 2 * cols, 2 * span), bf16),
            pltpu.VMEM((views * 2 * cols, 2 * rows), f32),
            pltpu.VMEM((levels - 1, views, 4, 2, cols, rows), bf16),
            pltpu.VMEM((levels - 1, views, 4, 2, cols, rows), bf16),
            pltpu.VMEM((3, views, 2, cols, rows), bf16),
            pltpu.VMEM((3, views, 2, cols, rows), bf16),
            pltpu.VMEM((BATCH, 2, 4 * cols, rows), f32),
            pltpu.VMEM((4 * cols, rows), f32),
            pltpu.VMEM((views, 3, 3 * cols, rows), f32),
            pltpu.VMEM((views, 2, 3, cols, rows), bf16),
            pltpu.VMEM((views, 2, 3, cols, rows), bf16),
            pltpu.VMEM((nt, 2, cols, rows), bf16),
            pltpu.VMEM((nt, 2, cols, rows), bf16),
            pltpu.VMEM((nv // 2, 2 * rows, views * 2 * cols), bf16),
            pltpu.VMEM((2, 2 * rows, span), f32),
            pltpu.VMEM((2, 2 * rows, span // 2), bf16),
            pltpu.VMEM((2, 2 * rows, span // 2), bf16),
            pltpu.VMEM((2, share_cols, depth, rows), f32),
            pltpu.VMEM((2, 2, depth, rows), bf16),
            pltpu.VMEM((2, 2, depth, rows), bf16),
            pltpu.VMEM((2, share_cols, depth, rows), bf16),
            dma((6 + views,)),
            dma((2, nv)),
            dma((nv // 2 - 1,)),
            dma((nv // 2 - 1,)),
            dma((2,)),
            dma((2,)),
            dma((levels - 1, views)),
            dma((levels - 1, views)),
            dma((3, views)),
            dma((3, views)),
            dma((views, 2)),
            dma((views, 2)),
            dma((views, 2 * levels)),
            dma((views, 2 * levels)),
            dma((views, 2 * levels)),
            dma((views, 2 * levels)),
            dma((views, nv // 2 - 1)),
            dma((views, nv // 2 - 1)),
            dma((2,)),
            dma((2,)),
            dma((2,)),
            dma((2,)),
            dma((7, 2, 3)),
            dma((7, 2, 3)),
        ],
        compiler_params=pltpu.CompilerParams(
            collective_id=0, has_side_effects=True, vmem_limit_bytes=FRONT_VMEM * MIB
        ),
        name="front",
    )(
        positions,
        live_counts.reshape(views),
        footprints.reshape(views),
        object_band,
        dual_band,
        probe_field,
        minus,
        plus,
        photon_counts,
        weights,
        volume,
    )
    return pl.pallas_call(
        widen_kernel,
        out_shape=(band, band, jax.ShapeDtypeStruct(volume.shape, f32)),
        in_specs=[vmem, vmem, hbm],
        out_specs=(vmem, vmem, hbm),
        scratch_shapes=[
            pltpu.VMEM(gathered.shape, bf16),
            pltpu.VMEM(gathered.shape, f32),
            dma((nv, 2)),
            dma((nv, 2)),
        ],
        compiler_params=pltpu.CompilerParams(vmem_limit_bytes=WIDEN_VMEM * MIB),
        name="widen",
    )(object_new, dual_new, gathered)


def solution(mesh):
    return jax.shard_map(
        functools.partial(per_device, mesh.shape["view"], mesh.shape["tile"]),
        mesh=mesh,
        in_specs=(
            P("view", None, "tile", None),
            P("view", None, "tile", None),
            P(),
            P("view", "tile"),
            P("view", "tile"),
            P("view", "tile", None, None),
            P("view", "tile"),
            P("view", None, "tile"),
            P(None, "tile", None, None),
        ),
        out_specs=(
            P("view", None, "tile", None),
            P("view", None, "tile", None),
            P(None, "tile", None, None),
        ),
        check_vma=False,
    )
```

```python
import functools

import jax
import jax.numpy as jnp
import numpy as np
from jax import lax
from jax.experimental import pallas as pl
from jax.experimental.pallas import tpu as pltpu
from jax.sharding import PartitionSpec as P

rho_weight = 0.5
step_size = 0.5
prior_weight = 0.5
MESH = pl.DeviceIdType.MESH
BATCH = 4
PIECE_ROWS = 16
FRONT_VMEM = 60
WIDEN_VMEM = 60
PUMP = (16, 6, 1, 2, 4, 4)
MIB = 2**20


def dft_tables(order):
    counter = np.arange(order)
    angles = ((counter[:, None] * counter[None, :]) % order).astype(np.float32)
    angles = angles * np.float32(2.0 * np.pi / order)
    scaling = np.float32(1.0 / np.sqrt(np.float32(order)))
    re, im = np.cos(angles) * scaling, -np.sin(angles) * scaling
    minus = np.block([[re, -im], [im, re]])
    plus = np.block([[re, im], [-im, re]])
    return jnp.asarray(minus, jnp.bfloat16), jnp.asarray(plus, jnp.bfloat16)


def phi(d):
    return d * lax.rsqrt(1.0 + d * d)


def flag(condition):
    return jnp.where(condition, jnp.float32(1.0), jnp.float32(0.0))


def dot(a, b):
    return jnp.dot(a, b, preferred_element_type=jnp.float32)


def front_kernel(
    nv,
    nt,
    positions,
    live_counts,
    footprints,
    object_hbm,
    dual_hbm,
    probe_hbm,
    minus_hbm,
    plus_hbm,
    counts_hbm,
    weights_hbm,
    volume_hbm,
    object_out,
    dual_out,
    gathered,
    probe,
    minus,
    plus,
    dual_v,
    reach,
    counts_v,
    weights_v,
    volume_v,
    weights_in,
    shadow,
    shadow_out,
    shadow_in,
    shared_out,
    shared_in,
    patch_tmp,
    power_tmp,
    acc,
    upd_out,
    upd_in,
    resid_first,
    resid_second,
    rt,
    grad,
    pair_out,
    pair_in,
    half,
    halo_out,
    halo_in,
    share,
    local_sem,
    chunk_sem,
    w_send,
    w_recv,
    obj_send,
    obj_recv,
    sh_send,
    sh_recv,
    gr_send,
    gr_recv,
    upd_send,
    upd_recv,
    res_send,
    res_recv,
    rel_send,
    rel_recv,
    rt_send,
    rt_recv,
    pair_send,
    pair_recv,
    halo_send,
    halo_recv,
    ag_send,
    ag_recv,
):
    v = lax.axis_index("view")
    t = lax.axis_index("tile")
    views, slots = positions.shape
    resid_full = (resid_first, resid_second)
    cols = reach.shape[2] // 3
    depth = volume_hbm.shape[2]
    share_cols = cols // nv
    span = share_cols * depth
    rows = probe.shape[2]
    pw = probe.shape[1]

    def remote(src, dst, send, recv, view, tile):
        return pltpu.make_async_remote_copy(
            src_ref=src,
            dst_ref=dst,
            send_sem=send,
            recv_sem=recv,
            device_id={"view": view, "tile": tile},
            device_id_type=MESH,
        )

    def view_at(k):
        return lax.rem(v + k + nv, nv)

    def tile_at(k):
        return lax.rem(t + k + nt, nt)

    group = 4
    levels = nt // group
    z, place = t // group, lax.rem(t, group)
    core = lax.rem(t, 2)
    sibling = t + 1 - 2 * core
    beside = t + 2 - 4 * (place // 2)
    view_x = lax.rem(v, 2)
    over = v + 1 - 2 * view_x

    def level_at(k):
        return lax.rem(z + k + levels, levels)

    back_v, back_t = view_at(-1), jnp.where(v == 0, tile_at(-1), t)
    fore_v, fore_t = view_at(1), jnp.where(v == nv - 1, tile_at(1), t)

    loads = [
        pltpu.make_async_copy(object_hbm, reach.at[:, :, pl.ds(0, cols), :], local_sem.at[0]),
        pltpu.make_async_copy(dual_hbm, dual_v, local_sem.at[1]),
    ]
    for a in range(views):
        loads.append(
            pltpu.make_async_copy(counts_hbm.at[a], counts_v.at[a], local_sem.at[2 + a])
        )
    for i, (source, target) in enumerate(
        ((probe_hbm, probe), (minus_hbm, minus), (plus_hbm, plus))
    ):
        loads.append(pltpu.make_async_copy(source, target, local_sem.at[2 + views + i]))

    def chunk_copies(c):
        first = pl.multiple_of(c * span, span)
        return (
            pltpu.make_async_copy(
                weights_hbm.at[:, :, pl.ds(first, span)],
                weights_v.at[:, :, pl.ds(first, span)],
                chunk_sem.at[0, c],
            ),
            pltpu.make_async_copy(
                volume_hbm.at[:, pl.ds(c * share_cols, share_cols)],
                volume_v.at[:, pl.ds(c * share_cols, share_cols)],
                chunk_sem.at[1, c],
            ),
        )

    loads[0].start()
    for c in range(nv):
        for copy in chunk_copies(c):
            copy.start()
    for copy in loads[1:]:
        copy.start()

    barrier = pltpu.get_barrier_semaphore()

    def greet(view, tile):
        pl.semaphore_signal(
            barrier, inc=1, device_id={"view": view, "tile": tile}, device_id_type=MESH
        )

    for k in range(1, nv):
        greet(view_at(k), t)
    for k in range(1, nt):
        greet(v, tile_at(k))
    greet(back_v, back_t)
    greet(fore_v, fore_t)
    pl.semaphore_wait(barrier, nv + nt)

    object_copies = [
        remote(
            object_hbm,
            reach.at[:, :, pl.ds(k * cols, cols), :],
            obj_send.at[k - 1],
            obj_recv.at[k - 1],
            v,
            tile_at(-k),
        )
        for k in (1, 2)
    ]
    for copy in object_copies:
        copy.start()

    peers = nv // 2 - 1
    piece_rows = PIECE_ROWS
    wide_span = 2 * span
    per_view = 2 * cols // piece_rows
    pieces = peers * views * per_view

    def pump(first, count):
        for extra in range(count):
            index = first + extra
            k = index % peers
            row_block = index // peers
            a = row_block // per_view
            rows_at = pl.multiple_of((row_block % per_view) * piece_rows, piece_rows)
            to = lax.rem(v + 2 * (k + 1), nv)
            first_voxel = pl.multiple_of((to // 2) * wide_span, wide_span)
            remote(
                weights_hbm.at[a, pl.ds(rows_at, piece_rows), pl.ds(first_voxel, wide_span)],
                weights_in.at[k, a, pl.ds(rows_at, piece_rows), :],
                w_send.at[k],
                w_recv.at[k],
                to,
                t,
            ).start()

    pumped = 0

    def pump_some(count):
        nonlocal pumped
        count = min(count, pieces - pumped)
        pump(pumped, count)
        pumped += count

    pump_some(PUMP[0])

    shadow[...] = jnp.zeros_like(shadow)

    def project(c, _):
        for copy in chunk_copies(c):
            copy.wait()
        first = pl.multiple_of(c * span, span)
        left = weights_v[:, :, pl.ds(first, span)].reshape(views * 2 * cols, span)
        block = volume_v[:, pl.ds(c * share_cols, share_cols)].astype(jnp.bfloat16)
        right = jnp.concatenate(
            [block[0].reshape(span, rows), block[1].reshape(span, rows)], axis=1
        )
        shadow[...] += dot(left, right)
        return 0

    lax.fori_loop(0, nv, project, 0)

    foot = [footprints[a] for a in range(views)]

    def shadow_part(a, k, part):
        first = a * 2 * cols + part * cols
        return shadow[first : first + cols, k * rows : (k + 1) * rows]

    def placed(to, a, k):
        return shadow_part(a, k, 0) * flag(foot[a] == to) + shadow_part(a, k, 1) * flag(
            foot[a] + 1 == to
        )

    def level_copy(k, a):
        return remote(
            shadow_out.at[k - 1, a],
            shadow_in.at[k - 1, a],
            sh_send.at[k - 1, a],
            sh_recv.at[k - 1, a],
            v,
            level_at(k) * group + place,
        )

    def group_copy(k, a):
        return remote(
            shared_out.at[k - 1, a],
            shared_in.at[k - 1, a],
            gr_send.at[k - 1, a],
            gr_recv.at[k - 1, a],
            v,
            z * group + lax.rem(place + k, group),
        )

    for a in range(views):
        for step in range(1, levels):
            for k in range(group):
                to = level_at(step) * group + k
                for plane in range(2):
                    shadow_out[step - 1, a, k, plane] = placed(to, a, plane).astype(jnp.bfloat16)
            level_copy(step, a).start()

    def level_sum(to, k, a, plane):
        total = placed(to, a, plane)
        for step in range(1, levels):
            total = total + shadow_in[step - 1, a, k, plane].astype(jnp.float32)
        return total

    def share_sums(a):
        for step in range(1, levels):
            level_copy(step, a).wait()
        for step in range(1, group):
            k = lax.rem(place + step, group)
            for plane in range(2):
                shared_out[step - 1, a, plane] = level_sum(z * group + k, k, a, plane).astype(
                    jnp.bfloat16
                )
            group_copy(step, a).start()

    pump_some(PUMP[1])

    for copy in loads[2 + views :]:
        copy.wait()
    probe_re, probe_im = probe[0], probe[1]
    acc[...] = jnp.zeros_like(acc)
    patch_tmp[...] = jnp.zeros_like(patch_tmp)
    power_tmp[...] = jnp.zeros_like(power_tmp)
    power_tmp[cols : cols + pw, :] = probe_re * probe_re + probe_im * probe_im
    for copy in loads[:2]:
        copy.wait()
    for copy in object_copies:
        copy.wait()
    for k in (1, 2):
        inside = flag(t + k < nt)
        for a in range(views):
            for plane in range(2):
                reach[a, plane, k * cols : (k + 1) * cols, :] = (
                    reach[a, plane, k * cols : (k + 1) * cols, :] * inside
                )

    def patches(a, b):
        base = b * BATCH
        offsets = [positions[a, base + j] for j in range(BATCH)]
        live_count = live_counts[a]
        lives = [flag(base + j < live_count) for j in range(BATCH)]
        re, im = probe[0], probe[1]
        exits = []
        for j in range(BATCH):
            obj_re = reach[a, 0, pl.ds(offsets[j], pw), :]
            obj_im = reach[a, 1, pl.ds(offsets[j], pw), :]
            exits.append(
                jnp.concatenate(
                    [re * obj_re - im * obj_im, re * obj_im + im * obj_re], axis=0
                ).astype(jnp.bfloat16)
            )
        done = dot(minus[...], jnp.concatenate(exits, axis=1)).astype(jnp.bfloat16)
        done = jnp.concatenate(
            [
                jnp.concatenate(
                    [
                        done[:pw, j * rows : (j + 1) * rows],
                        done[pw:, j * rows : (j + 1) * rows],
                    ],
                    axis=1,
                )
                for j in range(BATCH)
            ],
            axis=0,
        )
        spectrum = dot(done, plus[...])
        s_re, s_im = spectrum[:, :rows], spectrum[:, rows:]
        counts = counts_v[a, pl.ds(base, BATCH)].astype(jnp.float32).reshape(BATCH * pw, rows)
        power = 256.0 * (s_re * s_re + s_im * s_im) + 64.0
        factor = counts * lax.rsqrt(jnp.maximum(counts * power, 1e-20))
        replaced = jnp.concatenate([s_re * factor, s_im * factor], axis=1).astype(jnp.bfloat16)
        inverse = dot(replaced, minus[...]).astype(jnp.bfloat16)
        inverse = jnp.concatenate(
            [
                jnp.concatenate(
                    [
                        inverse[j * pw : (j + 1) * pw, :rows],
                        inverse[j * pw : (j + 1) * pw, rows:],
                    ],
                    axis=0,
                )
                for j in range(BATCH)
            ],
            axis=1,
        )
        wave = dot(plus[...], inverse)
        for j in range(BATCH):
            diff = wave[:, j * rows : (j + 1) * rows] - exits[j].astype(jnp.float32)
            d_re, d_im = diff[:pw] * lives[j], diff[pw:] * lives[j]
            patch_tmp[j, 0, cols : cols + pw, :] = re * d_re + im * d_im
            patch_tmp[j, 1, cols : cols + pw, :] = re * d_im - im * d_re
        for plane in range(2):
            total = acc[a, plane]
            for j in range(BATCH):
                total = total + patch_tmp[j, plane, pl.ds(cols - offsets[j], 3 * cols), :]
            acc[a, plane] = total
        total = acc[a, 2]
        for j in range(BATCH):
            total = total + power_tmp[pl.ds(cols - offsets[j], 3 * cols), :] * lives[j]
        acc[a, 2] = total

    def update_copy(a, k):
        return remote(
            upd_out.at[a, k - 1],
            upd_in.at[a, k - 1],
            upd_send.at[a, k - 1],
            upd_recv.at[a, k - 1],
            v,
            tile_at(k),
        )

    def run_patches(a, first, last):
        nonlocal pumped
        each = min(PUMP[2], (pieces - pumped) // (last - first))
        base = pumped

        def body(b, _):
            pump(base + (b - first) * each, each)
            patches(a, b)
            return 0

        lax.fori_loop(first, last, body, 0)
        pumped += each * (last - first)

    def send_update(a):
        for k in (1, 2):
            upd_out[a, k - 1] = acc[a, :, k * cols : (k + 1) * cols, :].astype(jnp.bfloat16)
            update_copy(a, k).start()

    from_one, from_two = flag(t >= 1), flag(t >= 2)

    def finish_object(a):
        for step in range(1, group):
            group_copy(step, a).wait()
        for k in (1, 2):
            update_copy(a, k).wait()
        upd = (
            acc[a, :, :cols, :]
            + upd_in[a, 0].astype(jnp.float32) * from_one
            + upd_in[a, 1].astype(jnp.float32) * from_two
        )
        scale = 1.0 / (1.0 + upd[2])
        for k in range(2):
            projection = level_sum(t, place, a, k)
            for step in range(1, group):
                projection = projection + shared_in[step - 1, a, k].astype(jnp.float32)
            obj = reach[a, k, :cols, :]
            dual = dual_v[a, k]
            new = obj + upd[k] * scale - rho_weight * (obj - projection - dual)
            object_out[a, k] = new
            dual_new = dual + projection - new
            dual_out[a, k] = dual_new
            resid_full[a][t, k] = dual_new.astype(jnp.bfloat16)

    def source_at(lane, tile):
        k, j = lane // 2, lane % 2
        base = lax.rem(tile // group - k + levels, levels) * group
        spot = lax.rem(tile, group)
        return base + (lax.rem(spot + 2, group) if j else spot)

    lanes = 2 * levels

    def resid_copy(a, lane, source, to):
        return remote(
            resid_full[a].at[source],
            resid_full[a].at[source],
            res_send.at[a, lane],
            res_recv.at[a, lane],
            v,
            to,
        )

    def relay_copy(a, lane, source):
        return remote(
            resid_full[a].at[source],
            resid_full[a].at[source],
            rel_send.at[a, lane],
            rel_recv.at[a, lane],
            v,
            sibling,
        )

    def send_resid(a):
        resid_copy(a, 1, t, beside).start()
        for k in range(1, levels):
            resid_copy(a, 2 * k, t, level_at(k) * group + place).start()
        relay_copy(a, 0, t).start()

    def relay_resid(a):
        resid_copy(a, 1, beside, beside).wait_recv()
        for k in range(1, levels):
            resid_copy(a, 2 * k + 1, beside, level_at(k) * group + place).start()
        relay_copy(a, 1, beside).start()
        for lane in range(2, lanes):
            source = source_at(lane, t)
            resid_copy(a, lane, source, t).wait_recv()
            relay_copy(a, lane, source).start()

    def rt_part(k, a):
        return rt.at[k, :, pl.ds(a * 2 * cols, 2 * cols)]

    def rt_copy(a, lane, to):
        return remote(
            rt_part(0, a),
            rt_part(lane, a),
            rt_send.at[a, lane - 1],
            rt_recv.at[a, lane - 1],
            to,
            t,
        )

    def send_windows(a):
        for lane in range(lanes):
            relay_copy(a, lane, source_at(lane, sibling)).wait_recv()
            relay_copy(a, lane, source_at(lane, t)).wait_send()
        for lane in range(1, lanes):
            resid_copy(a, lane, t, t).wait_send()
        for k in range(2):
            window = jnp.concatenate(
                [resid_full[a][foot[a], k], resid_full[a][foot[a] + 1, k]], axis=0
            )
            rt[0, k * rows : (k + 1) * rows, a * 2 * cols : (a + 1) * 2 * cols] = (
                window.astype(jnp.float32).T.astype(jnp.bfloat16)
            )
        for k in range(1, nv // 2):
            rt_copy(a, k, view_at(2 * k)).start()

    batches = slots // BATCH
    for a in range(views):
        loads[2 + a].wait()
        run_patches(a, 0, batches)
        send_update(a)
        share_sums(a)
    pump_some(PUMP[3])
    for a in range(views):
        finish_object(a)
        send_resid(a)
    pump_some(PUMP[4])
    for a in range(views):
        relay_resid(a)
    pump_some(PUMP[5])
    for a in range(views):
        send_windows(a)
    pump_some(pieces)

    base = pl.multiple_of((v // 2) * wide_span, wide_span)

    def product(lane, side):
        at = pl.multiple_of(side * span, span)
        if lane:
            block = weights_in[lane - 1, :, :, pl.ds(at, span)]
        else:
            block = weights_v[:, :, pl.ds(base + at, span)]
        return dot(rt[lane], block.reshape(views * 2 * cols, span))

    grad[0] = product(0, 1 - view_x)
    grad[1] = product(0, view_x)
    for lane in range(1, nv // 2):
        for a in range(views):
            rt_copy(a, lane, v).wait()
        remote(
            weights_hbm.at[:, :, pl.ds(0, wide_span)],
            weights_in.at[lane - 1],
            w_send.at[lane - 1],
            w_recv.at[lane - 1],
            v,
            t,
        ).wait()
        grad[0] += product(lane, 1 - view_x)
        if lane < nv // 2 - 1:
            grad[1] += product(lane, view_x)

    def pair_copy(part):
        return remote(
            pair_out.at[part], pair_in.at[part], pair_send.at[part], pair_recv.at[part], over, t
        )

    pair_parts = share_cols // 2
    part_span = 2 * depth
    for part in range(pair_parts):
        pair_out[part] = grad[0, :, part * part_span : (part + 1) * part_span].astype(jnp.bfloat16)
        pair_copy(part).start()
    grad[1] += product(nv // 2 - 1, view_x)
    def take_pair(part):
        pair_copy(part).wait()
        for c in (2 * part, 2 * part + 1):
            in_part = c * depth - part * part_span
            for k in range(2):
                both = grad[1, k * rows : (k + 1) * rows, c * depth : (c + 1) * depth] + pair_in[
                    part, k * rows : (k + 1) * rows, in_part : in_part + depth
                ].astype(jnp.float32)
                half[k, c] = volume_v[k, v * share_cols + c] - step_size * both.T

    row = lax.broadcasted_iota(jnp.int32, (depth, rows), 0)
    lane = lax.broadcasted_iota(jnp.int32, (depth, rows), 1)

    def inner(x):
        below = jnp.where(row == 0, 0.0, pltpu.roll(x, 1, 0))
        above = jnp.where(row == depth - 1, 0.0, pltpu.roll(x, depth - 1, 0))
        left = jnp.where(lane == 0, 0.0, pltpu.roll(x, 1, 1))
        right = jnp.where(lane == rows - 1, 0.0, pltpu.roll(x, rows - 1, 1))
        return phi(x - below) + phi(x - above) + phi(x - left) + phi(x - right)

    def finish(k, c, slot, before, after):
        x = half[k, c]
        prior = inner(x) + phi(x - before) + phi(x - after)
        share[k, slot] = (x - (step_size * prior_weight) * prior).astype(jnp.bfloat16)

    up, down, across = view_at(2), view_at(-2), view_at(4)
    other_up, other_down = lax.rem(over + 2, nv), lax.rem(over - 2 + nv, nv)
    other_across = lax.rem(over + 4, nv)
    spans = [pl.ds(2 * part, 2) for part in range(pair_parts)]
    sent = []

    def go(copy):
        copy.start()
        sent.append(copy)

    def hand_on(source, k, part, lane, to):
        return remote(
            gathered.at[source, k, spans[part]],
            gathered.at[source, k, spans[part]],
            ag_send.at[lane, k, part],
            ag_recv.at[lane, k, part],
            to,
            t,
        )

    def own(k, part, lane, to):
        return remote(
            share.at[k, spans[part]],
            gathered.at[v, k, spans[part]],
            ag_send.at[lane, k, part],
            ag_recv.at[lane, k, part],
            to,
            t,
        )

    def send_own(k, part):
        go(own(k, part, 0, up))
        go(own(k, part, 1, down))
        go(own(k, part, 2, over))

    def finish_inner(k, first, last):
        lax.fori_loop(
            first,
            last,
            lambda c, _: (finish(k, c, c - 1, half[k, c - 1], half[k, c + 1]), 0)[1],
            0,
        )

    take_pair(0)
    for part in range(1, pair_parts - 1):
        take_pair(part)
        for k in range(2):
            finish_inner(k, 2 * part - 1, 2 * part + 1)
            send_own(k, part - 1)
    take_pair(pair_parts - 1)
    for k in range(2):
        halo_out[0, k] = half[k, 0].astype(jnp.bfloat16)
        halo_out[1, k] = half[k, share_cols - 1].astype(jnp.bfloat16)
    halo_copies = [
        remote(halo_out.at[0], halo_in.at[1], halo_send.at[0], halo_recv.at[1], back_v, back_t),
        remote(halo_out.at[1], halo_in.at[0], halo_send.at[1], halo_recv.at[0], fore_v, fore_t),
    ]
    for copy in halo_copies:
        copy.start()
    for k in range(2):
        finish_inner(k, share_cols - 3, share_cols - 1)
        send_own(k, pair_parts - 2)
    for copy in halo_copies:
        copy.wait()
    has_back = flag((v > 0) | (t > 0))
    has_fore = flag((v < nv - 1) | (t < nt - 1))
    for k in range(2):
        finish(k, 0, share_cols - 2, halo_in[0, k].astype(jnp.float32) * has_back, half[k, 1])
        finish(
            k,
            share_cols - 1,
            share_cols - 1,
            half[k, share_cols - 2],
            halo_in[1, k].astype(jnp.float32) * has_fore,
        )
        send_own(k, pair_parts - 1)

    own_copy = pltpu.make_async_copy(share, gathered.at[v], local_sem.at[5 + views])
    own_copy.start()
    for part in range(pair_parts):
        for k in range(2):
            if k == 0:
                hand_on(down, 0, part, 0, up).wait_recv()
                go(hand_on(down, 0, part, 3, up))
            else:
                hand_on(up, 1, part, 1, down).wait_recv()
                go(hand_on(up, 1, part, 3, down))
            hand_on(over, k, part, 2, over).wait_recv()
            go(hand_on(over, k, part, 4, up))
            go(hand_on(over, k, part, 5, down))
    for part in range(pair_parts):
        for k in range(2):
            hand_on(across, k, part, 3, up).wait_recv()
            go(hand_on(across, k, part, 6, over))
    for part in range(pair_parts):
        hand_on(down, 1, part, 0, up).wait_recv()
        hand_on(up, 0, part, 1, up).wait_recv()
        for k in range(2):
            hand_on(other_down, k, part, 4, up).wait_recv()
            hand_on(other_up, k, part, 5, down).wait_recv()
            hand_on(other_across, k, part, 6, over).wait_recv()
    for copy in sent:
        copy.wait_send()
    own_copy.wait()


def widen_kernel(object_ref, dual_ref, gathered, object_out, dual_out, volume_out, low, wide, in_sem, out_sem):
    parts, _, share_cols = gathered.shape[:3]

    def load(i):
        return pltpu.make_async_copy(gathered.at[i], low.at[i], in_sem.at[i])

    def store(i):
        return pltpu.make_async_copy(
            wide.at[i], volume_out.at[:, pl.ds(i * share_cols, share_cols)], out_sem.at[i]
        )

    for i in range(parts):
        load(i).start()
    object_out[...] = object_ref[...]
    dual_out[...] = dual_ref[...]

    def step(i, _):
        load(i).wait()
        wide[i, :, 1 : share_cols - 1] = low[i, :, : share_cols - 2].astype(jnp.float32)
        wide[i, :, 0] = low[i, :, share_cols - 2].astype(jnp.float32)
        wide[i, :, share_cols - 1] = low[i, :, share_cols - 1].astype(jnp.float32)
        store(i).start()
        return 0

    lax.fori_loop(0, parts, step, 0)
    for i in range(parts):
        store(i).wait()


def per_device(
    nv,
    nt,
    object_band,
    dual_band,
    probe_field,
    positions,
    live_counts,
    photon_counts,
    footprints,
    weights,
    volume,
):
    views, _, cols, rows = object_band.shape
    pw = probe_field.shape[1]
    slots = positions.shape[1]
    depth = volume.shape[2]
    share_cols = cols // nv
    span = share_cols * depth
    minus, plus = dft_tables(pw)
    hbm = pl.BlockSpec(memory_space=pltpu.HBM)
    smem = pl.BlockSpec(memory_space=pltpu.SMEM)
    vmem = pl.BlockSpec(memory_space=pltpu.VMEM)
    bf16, f32 = jnp.bfloat16, jnp.float32
    dma = pltpu.SemaphoreType.DMA
    levels = nt // 4
    band = jax.ShapeDtypeStruct(object_band.shape, f32)
    object_new, dual_new, gathered = pl.pallas_call(
        functools.partial(front_kernel, nv, nt),
        out_shape=(
            band,
            band,
            jax.ShapeDtypeStruct((nv, 2, share_cols, depth, rows), bf16),
        ),
        in_specs=[smem] * 3 + [hbm] * 8,
        out_specs=(vmem, vmem, hbm),
        scratch_shapes=[
            pltpu.VMEM(probe_field.shape, f32),
            pltpu.VMEM(minus.shape, bf16),
            pltpu.VMEM(plus.shape, bf16),
            pltpu.VMEM((views, 2, cols, rows), f32),
            pltpu.VMEM((views, 2, 3 * cols, rows), f32),
            pltpu.VMEM((views, slots, pw, rows), jnp.int32),
            pltpu.VMEM(weights.shape, bf16),
            pltpu.VMEM(volume.shape, f32),
            pltpu.VMEM((nv // 2 - 1, views, 2 * cols, 2 * span), bf16),
            pltpu.VMEM((views * 2 * cols, 2 * rows), f32),
            pltpu.VMEM((levels - 1, views, 4, 2, cols, rows), bf16),
            pltpu.VMEM((levels - 1, views, 4, 2, cols, rows), bf16),
            pltpu.VMEM((3, views, 2, cols, rows), bf16),
            pltpu.VMEM((3, views, 2, cols, rows), bf16),
            pltpu.VMEM((BATCH, 2, 4 * cols, rows), f32),
            pltpu.VMEM((4 * cols, rows), f32),
            pltpu.VMEM((views, 3, 3 * cols, rows), f32),
            pltpu.VMEM((views, 2, 3, cols, rows), bf16),
            pltpu.VMEM((views, 2, 3, cols, rows), bf16),
            pltpu.VMEM((nt, 2, cols, rows), bf16),
            pltpu.VMEM((nt, 2, cols, rows), bf16),
            pltpu.VMEM((nv // 2, 2 * rows, views * 2 * cols), bf16),
            pltpu.VMEM((2, 2 * rows, span), f32),
            pltpu.VMEM((share_cols // 2, 2 * rows, 2 * depth), bf16),
            pltpu.VMEM((share_cols // 2, 2 * rows, 2 * depth), bf16),
            pltpu.VMEM((2, share_cols, depth, rows), f32),
            pltpu.VMEM((2, 2, depth, rows), bf16),
            pltpu.VMEM((2, 2, depth, rows), bf16),
            pltpu.VMEM((2, share_cols, depth, rows), bf16),
            dma((6 + views,)),
            dma((2, nv)),
            dma((nv // 2 - 1,)),
            dma((nv // 2 - 1,)),
            dma((2,)),
            dma((2,)),
            dma((levels - 1, views)),
            dma((levels - 1, views)),
            dma((3, views)),
            dma((3, views)),
            dma((views, 2)),
            dma((views, 2)),
            dma((views, 2 * levels)),
            dma((views, 2 * levels)),
            dma((views, 2 * levels)),
            dma((views, 2 * levels)),
            dma((views, nv // 2 - 1)),
            dma((views, nv // 2 - 1)),
            dma((share_cols // 2,)),
            dma((share_cols // 2,)),
            dma((2,)),
            dma((2,)),
            dma((7, 2, share_cols // 2)),
            dma((7, 2, share_cols // 2)),
        ],
        compiler_params=pltpu.CompilerParams(
            collective_id=0, has_side_effects=True, vmem_limit_bytes=FRONT_VMEM * MIB
        ),
        name="front",
    )(
        positions,
        live_counts.reshape(views),
        footprints.reshape(views),
        object_band,
        dual_band,
        probe_field,
        minus,
        plus,
        photon_counts,
        weights,
        volume,
    )
    return pl.pallas_call(
        widen_kernel,
        out_shape=(band, band, jax.ShapeDtypeStruct(volume.shape, f32)),
        in_specs=[vmem, vmem, hbm],
        out_specs=(vmem, vmem, hbm),
        scratch_shapes=[
            pltpu.VMEM(gathered.shape, bf16),
            pltpu.VMEM(gathered.shape, f32),
            dma((nv,)),
            dma((nv,)),
        ],
        compiler_params=pltpu.CompilerParams(vmem_limit_bytes=WIDEN_VMEM * MIB),
        name="widen",
    )(object_new, dual_new, gathered)


def solution(mesh):
    return jax.shard_map(
        functools.partial(per_device, mesh.shape["view"], mesh.shape["tile"]),
        mesh=mesh,
        in_specs=(
            P("view", None, "tile", None),
            P("view", None, "tile", None),
            P(),
            P("view", "tile"),
            P("view", "tile"),
            P("view", "tile", None, None),
            P("view", "tile"),
            P("view", None, "tile"),
            P(None, "tile", None, None),
        ),
        out_specs=(
            P("view", None, "tile", None),
            P("view", None, "tile", None),
            P(None, "tile", None, None),
        ),
        check_vma=False,
    )
```
